128 devices in a mesh: region: 8 (over x_hi, y), acq: 16 (over z, x_lo, core).
Axes of the slice: x: 4 (x_hi: 2, x_lo: 2; x = x_hi * 2 + x_lo), y: 4, z: 4, core: 2. Of those that a mesh axis runs over, the one named last changes fastest.
Arguments:
- scene_lines: bfloat16 [2, 128, 384, 512], P(None, 'acq', 'region'), may hold values from -20 to 20
- assigned_area: int32 [384, 1], P('region'), may hold values from 0 to 7; in each aligned block of 48 rows (0 to 47, 48 to 95, ...) at most 8 rows name the same one
Outputs:
- coherence: float32 [2, 128, 128, 4096], P(None, 'acq', None, 'region')
The draws below stay inside these ranges and needn't reach their ends.
Inputs may be any that keep to these rules, and one draw needn't show every extreme that they name: `assigned_area`: in every aligned block of 48 rows (the rows of one burst file) no region is named by more than 8 rows, a bound that some block reaches.
All inputs are finite; a program needn't handle non-finite values.
Results may differ from the reference program's by a relative error of at most 0.007.
Values may be sent and summed in bfloat16 or wider, within the bound.
A program may use at most 256 MiB of HBM per device.

```python
import math
import jax
import jax.numpy as jnp
import numpy as np
from jax import lax

SLANT_SAMPLES = 512
LINES_EACH_AREA = 8
ACQ_DEV = 8
EPOCH_TALLY = 128
ALONG_TRACK_LINES = 64
FILE_LINE_TALLY = 48
N_REGION = 8


def draw_scene_lines(key, part):
    key = jax.random.fold_in(key, 11)
    key_own, magnitude_seed = jax.random.split(key, 2)
    result_extent = (2, EPOCH_TALLY, N_REGION * FILE_LINE_TALLY, SLANT_SAMPLES)
    magnitude_entries = jnp.exp(jax.random.uniform(magnitude_seed, (1, EPOCH_TALLY, N_REGION * FILE_LINE_TALLY, 1), jnp.float32, -1.2, 1.2))
    values = magnitude_entries * jnp.clip(jax.random.normal(key_own, result_extent, jnp.float32), -6.0, 6.0)
    return values.astype(jnp.bfloat16)


def deal_out(rng, own, number, rows, amount, top, reach, skew):
    sequence = jax.random.permutation(rng, amount)
    heavy_load, common = shares(amount, rows * top, reach, skew, True), shares(amount, rows * top, reach, skew, False)
    places = jnp.arange(amount)

    def named(lengths, turn):
        used = int((lengths > 0).sum())
        fixed = max(1, used // 4)
        shifted = fixed + (places - fixed + turn * (used - fixed)) % max(1, amount - fixed)
        return jnp.zeros((amount,), jnp.int32).at[sequence[jnp.where(places < fixed, places, shifted)]].set(jnp.asarray(lengths, jnp.int32))

    lengths = jnp.where(number % 4 == 0, named(heavy_load, number // 4), named(common, number - number // 4 - 1))
    mixed = jax.random.permutation(jax.random.fold_in(own, 3), amount)
    donor, sink = mixed[0:amount // 2 * 2:2], mixed[1:amount // 2 * 2:2]
    room = jnp.minimum(lengths[donor] - 1, reach - lengths[sink]) // 2
    room = jnp.where((donor == sequence[0]) | (sink == sequence[0]) | (lengths[sink] == 0), 0, jnp.maximum(room, 0))
    shifted = jax.random.randint(jax.random.fold_in(own, 4), (amount // 2,), 0, 1 << 20) % (room + 1)
    lengths = lengths.at[donor].add(-shifted).at[sink].add(shifted)
    items = jnp.searchsorted(jnp.cumsum(lengths), jnp.arange(rows * top), side="right").astype(jnp.int32)
    listing = items.reshape(top, rows).T
    listing = listing[jax.random.permutation(jax.random.fold_in(own, 1), rows)]
    turn = jax.random.randint(jax.random.fold_in(own, 2), (rows, 1), 0, top)
    return jnp.take_along_axis(listing, (jnp.arange(top)[None, :] + turn) % top, axis=1)


def shares(count, total, bound, lean, full):
    loads = [(1 << 20) // math.isqrt(grade ** lean) + 1 for grade in range(1, count + 1)]
    largest = bound if full else min(bound, max(-(-total // count), total * loads[0] // sum(loads)))
    least = 1 if total - largest >= count - 1 else 0
    given, rest = [largest] + [least] * (count - 1), total - largest - least * (count - 1)
    while rest > 0:
        free = [i for i in range(1, count) if given[i] < largest] or [i for i in range(1, count) if given[i] < bound]
        mass, remaining = sum([loads[i] for i in free]), rest
        for i in free:
            extra = min(bound - given[i], max(1, remaining * loads[i] // mass), rest)
            given[i] = given[i] + extra
            rest = rest - extra
    return np.array(given)


def setup_inputs(seed: int = 0) -> dict:
    streams_of = jax.random.split(jax.random.key(seed), 3)
    scene_lines = draw_scene_lines(jax.random.fold_in(streams_of[2], 71), 0)
    assigned_area_keys = jax.random.split(jax.random.fold_in(streams_of[1], 1), (N_REGION * FILE_LINE_TALLY) // FILE_LINE_TALLY)
    assigned_area_turns = jax.random.permutation(jax.random.fold_in(streams_of[1], 3), (N_REGION * FILE_LINE_TALLY) // FILE_LINE_TALLY)
    assigned_area = jax.vmap(lambda own, number: deal_out(jax.random.fold_in(streams_of[1], 2), own, number, FILE_LINE_TALLY, N_REGION, 1, LINES_EACH_AREA, 2))(assigned_area_keys, assigned_area_turns).reshape((N_REGION * FILE_LINE_TALLY, 1))
    return dict(scene_lines=scene_lines, assigned_area=assigned_area)


def row_table(rows):
    index = jnp.arange(4, dtype=jnp.float32)
    taper = jnp.exp(-0.5 * ((index - 1.5) / 1.5) ** 2)
    taper = taper / jnp.sum(taper)
    rpos = jnp.arange(rows, dtype=jnp.int32)
    wins = jnp.arange(rows // 4, dtype=jnp.int32)
    values = taper[rpos % 4]
    return jnp.where(wins[:, None] == (rpos // 4)[None, :], values[None, :], jnp.float32(0.0))

def col_table(cols):
    index = jnp.arange(16, dtype=jnp.float32)
    taper = jnp.exp(-0.5 * ((index - 7.5) / 5.0) ** 2)
    taper = taper / jnp.sum(taper)
    cpos = jnp.arange(cols, dtype=jnp.int32)
    wins = jnp.arange(cols // 16, dtype=jnp.int32)
    values = taper[cpos % 16]
    table = jnp.where((cpos // 16)[:, None] == wins[None, :], values[:, None], jnp.float32(0.0))
    return table.astype(jnp.bfloat16)

def multilook(x, row_weights, col_weights):
    cols = jnp.einsum('...rc,cl->...rl', x.astype(jnp.float32), col_weights.astype(jnp.float32), precision=lax.Precision.HIGHEST)
    rowed = jnp.einsum('sr,...rl->...sl', row_weights, cols, precision=lax.Precision.HIGHEST)
    return rowed.reshape(rowed.shape[:-2] + (rowed.shape[-2] * rowed.shape[-1],))

def reference(scene_lines, assigned_area):
    overall_tally = assigned_area.shape[0]
    aimed_area = assigned_area[:, 0]
    membership_grid = (aimed_area[:, None] == jnp.arange(N_REGION, dtype=jnp.int32)[None, :]).astype(jnp.int32)
    tallied_lines = jnp.cumsum(membership_grid.reshape(N_REGION, FILE_LINE_TALLY, N_REGION), axis=1).reshape(overall_tally, N_REGION)
    worker_ordinal = lax.optimization_barrier(jnp.sum(membership_grid * tallied_lines, axis=1)) - 1
    scene_portion = jnp.arange(overall_tally, dtype=jnp.int32) // FILE_LINE_TALLY
    landing_line = aimed_area * ALONG_TRACK_LINES + scene_portion * LINES_EACH_AREA + worker_ordinal
    area_bands = jnp.zeros((2, EPOCH_TALLY, N_REGION * ALONG_TRACK_LINES, SLANT_SAMPLES), jnp.bfloat16).at[:, :, landing_line, :].set(scene_lines)
    row_weights = row_table(N_REGION * ALONG_TRACK_LINES)
    col_weights = col_table(SLANT_SAMPLES)
    real = area_bands[0].astype(jnp.float32)
    imag = area_bands[1].astype(jnp.float32)
    power = (real * real + imag * imag).astype(jnp.bfloat16)
    intensity = multilook(power, row_weights, col_weights)
    nblocks = EPOCH_TALLY // ACQ_DEV

    def one_first(i):
        pr = real[i]
        pim = imag[i]

        def one_block(bidx):
            start = (bidx * ACQ_DEV).astype(jnp.int32)
            qr = lax.dynamic_slice_in_dim(real, start, ACQ_DEV, 0)
            qi = lax.dynamic_slice_in_dim(imag, start, ACQ_DEV, 0)
            pre = pr[None] * qr + pim[None] * qi
            pim_part = pim[None] * qr - pr[None] * qi
            product = jnp.stack([pre, pim_part]).astype(jnp.bfloat16)
            looked = multilook(product, row_weights, col_weights)
            other = lax.dynamic_slice_in_dim(intensity, start, ACQ_DEV, 0)
            denom = jnp.sqrt(intensity[i][None, :] * other + 1e-06)
            return looked / denom[None]
        parts = lax.map(one_block, jnp.arange(nblocks, dtype=jnp.int32))
        return jnp.transpose(parts, (1, 0, 2, 3)).reshape(2, EPOCH_TALLY, -1)
    result = lax.map(one_first, jnp.arange(EPOCH_TALLY, dtype=jnp.int32))
    return jnp.transpose(result, (1, 0, 2, 3))
```

```python
import functools

import jax
import jax.numpy as jnp
from jax import lax
from jax.experimental import pallas as pl
from jax.experimental.pallas import tpu as pltpu
from jax.sharding import Mesh
from jax.sharding import PartitionSpec as P

F32 = jnp.float32
BF16 = jnp.bfloat16
NT = (((1,), (1,)), ((), ()))
GROUPS = ((0, 1), (2, 3))


def weight_tables():
    index = jnp.arange(4, dtype=F32)
    rows = jnp.exp(-0.5 * ((index - 1.5) / 1.5) ** 2)
    rows = rows / jnp.sum(rows)
    index = jnp.arange(16, dtype=F32)
    cols = jnp.exp(-0.5 * ((index - 7.5) / 5.0) ** 2)
    cols = (cols / jnp.sum(cols)).astype(BF16).astype(F32)
    c = jnp.arange(128, dtype=jnp.int32)
    mask = jnp.where(jnp.arange(8)[:, None] == (c // 16)[None, :], cols[c % 16][None, :], 0.0)
    return rows, mask.astype(F32)


def strip_sources(area):
    b = jnp.arange(48, dtype=jnp.int32)
    same = (area[:, None] == area[None, :]) & (b[None, :] < b[:, None])
    slot = area * 8 + jnp.sum(same.astype(jnp.int32), axis=1)
    match = (jnp.arange(64, dtype=jnp.int32)[:, None] == slot[None, :]).astype(jnp.int32)
    src = jnp.sum(match * b[None, :], axis=1)
    return src, jnp.sum(match, axis=1).astype(F32)


def build_own(src, fill, rows, mask, z0, lhs):
    def window(w, _):
        for r in range(4):
            s = w * 4 + r
            table = mask[...] * (rows[r] * fill[s])
            own = z0[src[s], pl.ds(0, 64), :].astype(F32)
            wide = own[:, None, :] * table[None, :, :]
            lhs[w, :, r * 128 : (r + 1) * 128] = wide.reshape(512, 128).astype(BF16)
        return 0

    lax.fori_loop(0, 16, window, 0)


def swap_parts(x):
    lane = lax.broadcasted_iota(jnp.int32, x.shape, x.ndim - 1)
    up = pltpu.roll(x, 120, axis=x.ndim - 1)
    down = pltpu.roll(x, 8, axis=x.ndim - 1)
    return jnp.where((lane // 8) % 2 == 0, up, down)


def window_coherence(w, src, fill, rows, mask, z, lhs, own_power, first):
    parts, powers = [], []
    for r in range(4):
        s = w * 4 + r
        row = z[src[s]]
        parts.append(row)
        wide = row.astype(F32)
        powers.append((wide * wide * (rows[r] * fill[s])).astype(BF16))
    data = jnp.concatenate(parts, axis=1)
    power = jnp.concatenate(powers, axis=1)
    looks = jnp.concatenate([mask[...].astype(BF16)] * 4, axis=1)
    halves = lax.dot_general(looks, power, NT, preferred_element_type=F32)
    lane = lax.broadcasted_iota(jnp.int32, (8, 128), 1)
    intensity = halves + swap_parts(halves)
    if first:
        for i in range(32):
            at = (i // 8) * 16 + i % 8
            own_power[w, i] = jnp.broadcast_to(intensity[:, at : at + 1], (8, 128))
    full = lax.dot_general(lhs[w], data, NT, preferred_element_type=F32)
    full = full.reshape(4, 2, 64, 128)
    sign = jnp.where((lane // 8) % 2 == 0, 1.0, -1.0).astype(F32)
    re_rows = full[:, 0].reshape(32, 8, 128)
    im_rows = full[:, 1].reshape(256, 128)
    total = swap_parts(im_rows).reshape(32, 8, 128) + sign[None] * re_rows
    scale = lax.rsqrt(own_power[w] * intensity[None] + 1e-6)
    return total * scale


def pairs_kernel(src, fill, rows, mask, z, out, lhs, own_power):
    build_own(src, fill, rows, mask, z.at[0], lhs)
    for g in range(2):

        def region(o, _):
            both = [
                window_coherence(o * 2 + h, src, fill, rows, mask, z.at[g], lhs, own_power, g == 0)
                for h in range(2)
            ]
            both = jnp.stack(both, axis=1).reshape(4, 8, 16, 128)
            out[o, :, g] = both.astype(BF16)
            return 0

        lax.fori_loop(0, 8, region, 0)


def finish_kernel(recv, out):
    z = lax.axis_index("z")
    for g in range(2):
        x = recv[:, g, 0].astype(F32)
        x = x.reshape(8, 4, 2, 8, 128)
        x = jnp.swapaxes(x, 1, 2).reshape(512, 128)
        y = x.T
        for d in range(2):
            at = lax.rem(z + GROUPS[g][d], 4) * 32
            for q in range(4):
                for part in range(2):
                    k = d * 64 + q * 16 + part * 8
                    out[part, 0, pl.ds(pl.multiple_of(at + q * 8, 8), 8), :] = y[k : k + 8]


def local(scene_lines, assigned_area):
    rows, mask = weight_tables()
    src, fill = strip_sources(assigned_area[:, 0])
    staged = scene_lines.reshape(2, 8, 48, 4, 128).transpose(3, 2, 0, 1, 4).reshape(4, 48, 16, 128)
    tiles = lax.all_to_all(staged, ("x_lo", "core"), 0, 0, tiled=True)
    every = lax.all_gather(tiles, "z")
    z = lax.axis_index("z")
    every = jnp.roll(every, -z, axis=0)
    every = every.reshape(2, 8, 48, 16, 128).transpose(0, 2, 1, 3, 4).reshape(2, 48, 128, 128)
    smem = pl.BlockSpec(memory_space=pltpu.SMEM)
    vmem = pl.BlockSpec(memory_space=pltpu.VMEM)
    sent = pl.pallas_call(
        pairs_kernel,
        out_shape=jax.ShapeDtypeStruct((8, 4, 2, 8, 16, 128), BF16),
        in_specs=[smem, smem, smem, vmem, vmem],
        out_specs=vmem,
        scratch_shapes=[pltpu.VMEM((16, 512, 512), BF16), pltpu.VMEM((16, 32, 8, 128), F32)],
        compiler_params=pltpu.CompilerParams(vmem_limit_bytes=48 << 20),
    )(src, fill, rows, mask, every)
    sent = sent.reshape(32, 2, 8, 16, 128)
    got = lax.all_to_all(sent, ("x_hi", "y", "x_lo", "core"), 0, 0, tiled=True)
    return pl.pallas_call(
        finish_kernel,
        grid=(8,),
        out_shape=jax.ShapeDtypeStruct((2, 8, 128, 512), F32),
        in_specs=[pl.BlockSpec((32, 2, 1, 16, 128), lambda i: (0, 0, i, 0, 0))],
        out_specs=pl.BlockSpec((2, 1, 128, 512), lambda i: (0, i, 0, 0)),
        compiler_params=pltpu.CompilerParams(vmem_limit_bytes=32 << 20),
    )(got)


def solution(mesh):
    fine = Mesh(mesh.devices.reshape(2, 4, 4, 2, 2), ("x_hi", "y", "z", "x_lo", "core"))
    region, acq = ("x_hi", "y"), ("z", "x_lo", "core")
    placed = (P(None, acq, region, None), P(region, None))
    return jax.shard_map(
        local, mesh=fine, in_specs=placed, out_specs=P(None, acq, None, region), check_vma=False
    )
```

```python
import jax
import jax.numpy as jnp
import numpy as np
from jax import lax
from jax.experimental import pallas as pl
from jax.experimental.pallas import tpu as pltpu
from jax.sharding import PartitionSpec as P

F32 = jnp.float32
BF16 = jnp.bfloat16
NT = (((1,), (1,)), ((), ()))
MESH = pl.DeviceIdType.MESH


def taper(length, centre, width):
    index = np.arange(length, dtype=np.float32)
    values = np.exp(np.float32(-0.5) * ((index - np.float32(centre)) / np.float32(width)) ** 2)
    return values / np.sum(values)


ROWS = [float(v) for v in taper(4, 1.5, 1.5)]
COLS = [float(v) for v in taper(16, 7.5, 5.0).astype(jnp.bfloat16).astype(np.float32)]


def look_mask():
    look = lax.broadcasted_iota(jnp.int32, (8, 128), 0)
    col = lax.broadcasted_iota(jnp.int32, (8, 128), 1)
    values = jnp.zeros((8, 128), F32)
    for k in range(16):
        values = jnp.where(col % 16 == k, COLS[k], values)
    return jnp.where(look == col // 16, values, 0.0)


def strip_sources(area):
    b = jnp.arange(48, dtype=jnp.int32)
    same = (area[:, None] == area[None, :]) & (b[None, :] < b[:, None])
    slot = area * 8 + jnp.sum(same.astype(jnp.int32), axis=1)
    match = (jnp.arange(64, dtype=jnp.int32)[:, None] == slot[None, :]).astype(jnp.int32)
    src = jnp.sum(match * b[None, :], axis=1)
    return src, jnp.sum(match, axis=1).astype(F32)


def swap_parts(x):
    lane = lax.broadcasted_iota(jnp.int32, x.shape, x.ndim - 1)
    up = pltpu.roll(x, 120, axis=x.ndim - 1)
    down = pltpu.roll(x, 8, axis=x.ndim - 1)
    return jnp.where((lane // 8) % 2 == 0, up, down)


def build_own(src, fill, mask, z0, lhs):
    def window(w, _):
        for r in range(4):
            s = w * 4 + r
            table = mask * (ROWS[r] * fill[s])
            own = z0[src[s]].astype(F32)
            wide = own[:, None, :] * table[None, :, :]
            lhs[w, :, r * 128 : (r + 1) * 128] = wide.reshape(512, 128).astype(BF16)
        return 0

    lax.fori_loop(0, 16, window, 0)


def window_sums(w, src, fill, looks, z, lhs):
    parts, powers = [], []
    for r in range(4):
        s = w * 4 + r
        row = z[src[s]]
        parts.append(row)
        wide = row.astype(F32)
        powers.append((wide * wide * (ROWS[r] * fill[s])).astype(BF16))
    data = jnp.concatenate(parts, axis=1)
    power = jnp.concatenate(powers, axis=1)
    halves = lax.dot_general(looks, power, NT, preferred_element_type=F32)
    full = lax.dot_general(lhs[w], data, NT, preferred_element_type=F32)
    return full, halves


def coherence(full, halves, own):
    lane = lax.broadcasted_iota(jnp.int32, (8, 128), 1)
    intensity = halves + swap_parts(halves)
    full = full.reshape(4, 2, 64, 128)
    sign = jnp.where((lane // 8) % 2 == 0, 1.0, -1.0).astype(F32)
    re_rows = full[:, 0].reshape(32, 8, 128)
    im_rows = full[:, 1].reshape(256, 128)
    total = swap_parts(im_rows).reshape(32, 8, 128) + sign[None] * re_rows
    return total * lax.rsqrt(own * intensity[None] + 1e-6)


def pairs_kernel(
    src, fill, staged, recv0, recv1, recv2,
    z0, z1, z2, lhs, own_power, res0, res1, res2,
    own_sem, a_send, a_recv, b_send, b_recv, c_send, c_recv,
):
    k = lax.axis_index("region")
    acq = lax.axis_index("acq")
    z = acq // 4
    q = acq % 4
    xl, core = q // 2, q % 2
    right = (k, ((z + 1) % 4) * 4 + q)
    left = (k, ((z + 3) % 4) * 4 + q)

    def tile(j):
        return ((xl + j // 2) % 2) * 2 + (core + j % 2) % 2

    def rows16(start):
        return pl.ds(pl.multiple_of(start, 16), 16)

    barrier = pltpu.get_barrier_semaphore()
    for peer in (left, right):
        pl.semaphore_signal(barrier, inc=1, device_id=peer, device_id_type=MESH)

    def greet(n, _):
        o, p = n // 4, n % 4

        @pl.when(jnp.logical_or(o != k, p != q))
        def _():
            pl.semaphore_signal(barrier, inc=1, device_id=(o, z * 4 + p), device_id_type=MESH)

        return 0

    lax.fori_loop(0, 32, greet, 0)
    pl.semaphore_wait(barrier, 33)

    def remote(from_ref, to_ref, send, recv, peer):
        return pltpu.make_async_remote_copy(
            src_ref=from_ref, dst_ref=to_ref, send_sem=send, recv_sem=recv,
            device_id=peer, device_id_type=MESH,
        )

    a_copies = {}
    for j in (1, 2, 3):
        to = tile(j)
        a_copies[j] = remote(
            staged.at[to], z0.at[:, rows16(q * 16), :], a_send.at[j], a_recv.at[j], (k, z * 4 + to)
        )
        a_copies[j].start()
    own = pltpu.make_async_copy(staged.at[q], z0.at[:, rows16(q * 16), :], own_sem)
    own.start()

    b_copies = {}

    def send_along(j):
        t = tile(j)
        data = staged.at[q] if j == 0 else z0.at[:, rows16(t * 16), :]
        b_copies[j, 0] = remote(
            data, z1.at[:, rows16(t * 16), :], b_send.at[j], b_recv.at[j], right
        )
        b_copies[j, 1] = remote(
            data, z1.at[:, rows16(64 + t * 16), :], b_send.at[4 + j], b_recv.at[4 + j], left
        )
        b_copies[j, 0].start()
        b_copies[j, 1].start()

    send_along(0)
    for j in (1, 2, 3):
        a_copies[j].wait_recv()
        send_along(j)
    own.wait()

    mask = look_mask()
    looks = jnp.concatenate([mask.astype(BF16)] * 4, axis=1)
    build_own(src, fill, mask, z0, lhs)

    def send_results(o, g, res, recv):
        for p in range(4):
            here = jnp.logical_and(o == k, q == p)
            block, land = res.at[o * 4 + p], recv.at[k * 4 + q]

            @pl.when(here)
            def _():
                pltpu.make_async_copy(block, land, c_recv.at[g]).start()

            @pl.when(jnp.logical_not(here))
            def _():
                remote(block, land, c_send.at[g], c_recv.at[g], (o, z * 4 + p)).start()

    lane = lax.broadcasted_iota(jnp.int32, (8, 128), 1)

    def small_group(g, data, res, recv):
        def region(n, _):
            o = (k + n) % 8
            full, halves = [], []
            for h in range(2):
                f, p = window_sums(o * 2 + h, src, fill, looks, data, lhs)
                full.append(f)
                halves.append(p)
            full = jnp.concatenate(full, axis=1)
            halves = jnp.concatenate(halves, axis=1)
            if g == 0:
                intensity = halves + swap_parts(halves)
                for h in range(2):
                    for i in range(32):
                        at = h * 64 + (i // 8) * 16 + i % 8
                        own_power[o * 2 + h, i] = jnp.broadcast_to(
                            intensity[:, at : at + 1], (8, 128)
                        )
            own = jnp.where((lane < 64)[None], own_power[o * 2], own_power[o * 2 + 1])
            both = coherence(full, halves, own).reshape(4, 4, 16, 128)
            res[pl.ds(o * 4, 4)] = both.astype(BF16)
            send_results(o, g, res, recv)
            return 0

        lax.fori_loop(0, 8, region, 0)

    def large_group(g, data, res, recv):
        def region(n, _):
            o = (k + n) % 8
            both = []
            for h in range(2):
                full, halves = window_sums(o * 2 + h, src, fill, looks, data, lhs)
                both.append(coherence(full, halves, own_power[o * 2 + h]))
            both = jnp.stack(both, axis=1).reshape(4, 8, 16, 128)
            res[pl.ds(o * 4, 4)] = both.astype(BF16)
            send_results(o, g, res, recv)
            return 0

        lax.fori_loop(0, 8, region, 0)

    small_group(0, z0, res0, recv0)

    relays = []
    for j in (0, 1):
        b_copies[j, 0].wait_recv()
        t = tile(j)
        relays.append(remote(
            z1.at[:, rows16(t * 16), :], z2.at[:, rows16(t * 16), :],
            b_send.at[8 + j], b_recv.at[8 + j], right,
        ))
        relays[-1].start()
    for j in (2, 3):
        b_copies[j, 1].wait_recv()
        t = tile(j)
        relays.append(remote(
            z1.at[:, rows16(64 + t * 16), :], z2.at[:, rows16(t * 16), :],
            b_send.at[8 + j], b_recv.at[8 + j], left,
        ))
        relays[-1].start()
    for j in (2, 3):
        b_copies[j, 0].wait_recv()
    for j in (0, 1):
        b_copies[j, 1].wait_recv()
    large_group(1, z1, res1, recv1)

    for relay in relays:
        relay.wait_recv()
    small_group(2, z2, res2, recv2)

    for j in (1, 2, 3):
        a_copies[j].wait_send()
    for copy in b_copies.values():
        copy.wait_send()
    for relay in relays:
        relay.wait_send()
    for g, (res, recv) in enumerate(((res0, recv0), (res1, recv1), (res2, recv2))):
        some = pl.ds(0, 31)
        pltpu.make_async_copy(res.at[some], recv.at[some], c_send.at[g]).wait()
        pltpu.make_async_copy(res, recv, c_recv.at[g]).wait()


def finish_kernel(recv0, recv1, recv2, out):
    z = lax.axis_index("acq") // 4
    lane = lax.broadcasted_iota(jnp.int32, (8, 128), 1)
    low = (lane < 64)[None]

    def place(x, offsets, i):
        y = x.reshape(512, 128).T
        for d, offset in enumerate(offsets):
            at = ((z + offset) % 4) * 32
            for q in range(4):
                for part in range(2):
                    n = d * 64 + q * 16 + part * 8
                    out[part, i, pl.ds(pl.multiple_of(at + q * 8, 8), 8), :] = y[n : n + 8]

    for i in range(2):
        a = recv0[:, 0].astype(F32).reshape(32, 2, 8, 128)[:, i]
        b = recv2[:, 0].astype(F32).reshape(32, 2, 8, 128)[:, i]
        turned_a = pltpu.roll(a.reshape(256, 128), 64, axis=1).reshape(32, 8, 128)
        turned_b = pltpu.roll(b.reshape(256, 128), 64, axis=1).reshape(32, 8, 128)
        first = jnp.where(low, a, turned_b).reshape(8, 4, 8, 128)
        second = jnp.where(low, turned_a, b).reshape(8, 4, 8, 128)
        place(jnp.stack([first, second], axis=1), (0, 2), i)
        c = recv1[:, i].astype(F32).reshape(8, 4, 2, 8, 128)
        place(jnp.swapaxes(c, 1, 2), (3, 1), i)


def local(scene_lines, assigned_area):
    src, fill = strip_sources(assigned_area[:, 0])
    staged = scene_lines.reshape(2, 8, 48, 4, 128).transpose(3, 2, 0, 1, 4).reshape(4, 48, 16, 128)
    smem = pl.BlockSpec(memory_space=pltpu.SMEM)
    vmem = pl.BlockSpec(memory_space=pltpu.VMEM)
    hbm = pl.BlockSpec(memory_space=pl.ANY)
    small, large = (32, 4, 16, 128), (32, 8, 16, 128)
    got = pl.pallas_call(
        pairs_kernel,
        out_shape=[jax.ShapeDtypeStruct(shape, BF16) for shape in (small, large, small)],
        in_specs=[smem, smem, vmem],
        out_specs=[hbm, hbm, hbm],
        scratch_shapes=[
            pltpu.VMEM((48, 64, 128), BF16),
            pltpu.VMEM((48, 128, 128), BF16),
            pltpu.VMEM((48, 64, 128), BF16),
            pltpu.VMEM((16, 512, 512), BF16),
            pltpu.VMEM((16, 32, 8, 128), F32),
            pltpu.VMEM(small, BF16),
            pltpu.VMEM(large, BF16),
            pltpu.VMEM(small, BF16),
            pltpu.SemaphoreType.DMA,
            pltpu.SemaphoreType.DMA((4,)),
            pltpu.SemaphoreType.DMA((4,)),
            pltpu.SemaphoreType.DMA((12,)),
            pltpu.SemaphoreType.DMA((12,)),
            pltpu.SemaphoreType.DMA((3,)),
            pltpu.SemaphoreType.DMA((3,)),
        ],
        compiler_params=pltpu.CompilerParams(
            vmem_limit_bytes=40 << 20, collective_id=0, has_side_effects=True
        ),
    )(src, fill, staged)
    return pl.pallas_call(
        finish_kernel,
        grid=(4,),
        out_shape=jax.ShapeDtypeStruct((2, 8, 128, 512), F32),
        in_specs=[
            pl.BlockSpec((32, 1, 16, 128), lambda i: (0, i, 0, 0)),
            pl.BlockSpec((32, 2, 16, 128), lambda i: (0, i, 0, 0)),
            pl.BlockSpec((32, 1, 16, 128), lambda i: (0, i, 0, 0)),
        ],
        out_specs=pl.BlockSpec((2, 2, 128, 512), lambda i: (0, i, 0, 0)),
        compiler_params=pltpu.CompilerParams(vmem_limit_bytes=32 << 20),
    )(*got)


def solution(mesh):
    placed = (P(None, "acq", "region", None), P("region", None))
    return jax.shard_map(
        local, mesh=mesh, in_specs=placed, out_specs=P(None, "acq", None, "region"), check_vma=False
    )
```

```python
import jax
import jax.numpy as jnp
import numpy as np
from jax import lax
from jax.experimental import pallas as pl
from jax.experimental.pallas import tpu as pltpu
from jax.sharding import PartitionSpec as P

F32 = jnp.float32
BF16 = jnp.bfloat16
NT = (((1,), (1,)), ((), ()))
MESH = pl.DeviceIdType.MESH


def taper(length, centre, width):
    index = np.arange(length, dtype=np.float32)
    values = np.exp(np.float32(-0.5) * ((index - np.float32(centre)) / np.float32(width)) ** 2)
    return values / np.sum(values)


ROWS = [float(v) for v in taper(4, 1.5, 1.5)]
COLS = [float(v) for v in taper(16, 7.5, 5.0).astype(jnp.bfloat16).astype(np.float32)]


def lanes(shape):
    return lax.broadcasted_iota(jnp.int32, shape, len(shape) - 1)


def column_weights():
    col = lanes((8, 128))
    values = jnp.zeros((8, 128), F32)
    for k in range(16):
        values = jnp.where(col % 16 == k, COLS[k], values)
    return values


def swap_parts(x):
    up = pltpu.roll(x, 120, axis=x.ndim - 1)
    down = pltpu.roll(x, 8, axis=x.ndim - 1)
    return jnp.where((lanes(x.shape) // 8) % 2 == 0, up, down)


def sort_rows(area, table):
    slot = lanes((8, 128))
    owner, place = slot // 8, slot % 8
    source = jnp.zeros((8, 128), jnp.int32)
    held = jnp.zeros((8, 128), jnp.int32)
    count = jnp.zeros((8, 128), jnp.int32)
    for b in range(48):
        hit = owner == area[b, 0]
        take = jnp.logical_and(hit, count == place)
        source = jnp.where(take, b, source)
        held = jnp.where(take, 1, held)
        count = count + hit.astype(jnp.int32)
    table[0] = source
    table[1] = held


def stage_columns(scene, wide, staged):
    for part in range(2):
        for a in range(8):
            n = part * 8 + a
            x = scene[part, a].astype(F32)
            for c in range(4):
                wide[c, n * 48 : (n + 1) * 48, :] = x[:, c * 128 : (c + 1) * 128]

    def row(b, _):
        for c in range(4):
            staged[c, b] = wide[c, pl.ds(b, 16, stride=48), :].astype(BF16)
        return 0

    lax.fori_loop(0, 48, row, 0, unroll=4)


def build_own(w, src, weights, z0, lhs):
    look = (lanes((8, 128)) // 16) % 4
    for r in range(4):
        s = w * 4 + r
        table = weights * (ROWS[r] * src[1, 0, s].astype(F32))
        own = z0[src[0, 0, s]].astype(F32).reshape(4, 2, 8, 128)
        tables = [jnp.where(look == l, table, 0.0) for l in range(4)]
        spread = jnp.stack([own * t[None, None] for t in tables], axis=1)
        lhs[w, :, r * 128 : (r + 1) * 128] = spread.reshape(256, 128).astype(BF16)


def window_sums(w, src, weights, z, lhs):
    zero = jnp.zeros((64, 128), BF16)
    low = lanes((64, 128)) < 64
    look = (lanes((8, 128)) // 16) % 4 == lax.broadcasted_iota(jnp.int32, (8, 128), 0)
    data, power, looks = [], [], []
    for r in range(4):
        s = w * 4 + r
        row = z[src[0, 0, s]]
        square = row * row
        data.append(jnp.concatenate([jnp.where(low, row, zero), jnp.where(low, zero, row)], axis=0))
        power.append(
            jnp.concatenate([jnp.where(low, square, zero), jnp.where(low, zero, square)], axis=0)
        )
        table = weights * (ROWS[r] * src[1, 0, s].astype(F32))
        looks.append(jnp.where(look, table, 0.0).astype(BF16))
    data = jnp.concatenate(data, axis=1)
    power = jnp.concatenate(power, axis=1)
    looks = jnp.concatenate(looks, axis=1)
    full = lax.dot_general(lhs[w], data, NT, preferred_element_type=F32)
    halves = lax.dot_general(looks, power, NT, preferred_element_type=F32)
    return full, halves + swap_parts(halves)


def own_intensities(w, intensity, own_power):
    turned = intensity.T
    low = lanes((8, 128)) < 64
    for q in range(4):
        for l in range(4):
            first = jnp.broadcast_to(turned[q * 16 : q * 16 + 8, l : l + 1], (8, 128))
            second = jnp.broadcast_to(turned[64 + q * 16 : 72 + q * 16, l : l + 1], (8, 128))
            own_power[w, q * 4 + l] = jnp.where(low, first, second)


def coherence(full, intensity, own):
    full = full.reshape(16, 2, 8, 128)
    sign = jnp.where((lanes((8, 128)) // 8) % 2 == 0, 1.0, -1.0).astype(F32)
    swapped = swap_parts(full[:, 1].reshape(128, 128)).reshape(16, 8, 128)
    total = swapped + sign[None] * full[:, 0]
    other = jnp.stack([jnp.broadcast_to(intensity[l : l + 1], (8, 128)) for l in range(4)], axis=0)
    product = own.reshape(4, 4, 8, 128) * other[None]
    scale = lax.rsqrt(product + 1e-6)
    return (total.reshape(4, 4, 8, 128) * scale).reshape(4, 2, 16, 128).astype(BF16)


def pairs_kernel(
    area, scene, recv,
    wide, staged, table, src, z0, z1, z2, z3, lhs, own_power, res,
    local_sem, a_send, a_recv, b_send, b_recv, c_send, c_recv,
):
    zs = (z0, z1, z2, z3)
    k = lax.axis_index("region")
    acq = lax.axis_index("acq")
    z = acq // 4
    q = acq % 4
    xl, core = q // 2, q % 2
    right = (k, ((z + 1) % 4) * 4 + q)
    left = (k, ((z + 3) % 4) * 4 + q)

    def tile(j):
        return ((xl + j // 2) % 2) * 2 + (core + j % 2) % 2

    def rows16(start):
        return pl.ds(pl.multiple_of(start, 16), 16)

    barrier = pltpu.get_barrier_semaphore()
    for peer in (left, right):
        pl.semaphore_signal(barrier, inc=1, device_id=peer, device_id_type=MESH)

    def greet(n, _):
        o, p = n // 4, n % 4

        @pl.when(jnp.logical_or(o != k, p != q))
        def _():
            pl.semaphore_signal(barrier, inc=1, device_id=(o, z * 4 + p), device_id_type=MESH)

        return 0

    lax.fori_loop(0, 32, greet, 0)

    sort_rows(area, table)
    sorted_rows = pltpu.make_async_copy(table, src, local_sem.at[0])
    sorted_rows.start()
    stage_columns(scene, wide, staged)
    pl.semaphore_wait(barrier, 33)

    def remote(from_ref, to_ref, send, recv, peer):
        return pltpu.make_async_remote_copy(
            src_ref=from_ref, dst_ref=to_ref, send_sem=send, recv_sem=recv,
            device_id=peer, device_id_type=MESH,
        )

    a_copies = {}
    for j in (2, 3, 1):
        to = tile(j)
        a_copies[j] = remote(
            staged.at[to], zs[0].at[:, rows16(q * 16), :], a_send.at[j], a_recv.at[j],
            (k, z * 4 + to),
        )
        a_copies[j].start()

    def near(j, side):
        return zs[1 + j // 2].at[:, rows16(side * 32 + ((core + j) % 2) * 16), :]

    b_copies = {}

    def send_along(j):
        data = staged.at[q] if j == 0 else zs[0].at[:, rows16(tile(j) * 16), :]
        for side, peer in ((0, right), (1, left)):
            n = side * 4 + j
            b_copies[j, side] = remote(data, near(j, side), b_send.at[n], b_recv.at[n], peer)
            b_copies[j, side].start()

    send_along(0)
    own = pltpu.make_async_copy(staged.at[q], zs[0].at[:, rows16(q * 16), :], local_sem.at[1])
    own.start()
    for j in (1, 2, 3):
        a_copies[j].wait_recv()
        send_along(j)
    own.wait()
    sorted_rows.wait()

    weights = column_weights()

    def send_results(o, g):
        for p in range(4):
            here = jnp.logical_and(o == k, q == p)
            block, land = res.at[g, o * 4 + p], recv.at[g, k * 4 + q]

            @pl.when(here)
            def _():
                pltpu.make_async_copy(block, land, c_recv.at[g]).start()

            @pl.when(jnp.logical_not(here))
            def _():
                remote(block, land, c_send.at[g], c_recv.at[g], (o, z * 4 + p)).start()

    def group(g):
        def step(n, _):
            regions = (
                ((k // 4 + n) % 2) * 4 + (k + n + 1) % 4,
                ((k // 4 + n + 1) % 2) * 4 + (k + n + 3) % 4,
            )
            if g == 0:
                for o in regions:
                    for h in range(2):
                        build_own(o * 2 + h, src, weights, zs[0], lhs)
            sums = [
                window_sums(o * 2 + h, src, weights, zs[g], lhs)
                for o in regions
                for h in range(2)
            ]
            if g == 0:
                for m, o in enumerate(regions):
                    for h in range(2):
                        own_intensities(o * 2 + h, sums[m * 2 + h][1], own_power)
            for m, o in enumerate(regions):
                for h in range(2):
                    full, intensity = sums[m * 2 + h]
                    block = coherence(full, intensity, own_power[o * 2 + h])
                    res[g, pl.ds(o * 4, 4), h * 2 : h * 2 + 2] = block
                send_results(o, g)
            return 0

        lax.fori_loop(0, 4, step, 0)

    group(0)
    for j in (0, 1):
        for side in range(2):
            b_copies[j, side].wait_recv()
    group(1)

    relays = []

    def relay(j):
        side, peer = ((0, right), (0, right), (1, left), (1, left))[j]
        n = 8 + j
        relays.append(remote(
            near(j, side), zs[3].at[:, rows16(tile(j) * 16), :], b_send.at[n], b_recv.at[n], peer
        ))
        relays[-1].start()

    relay(0)
    relay(1)
    for j in (2, 3):
        b_copies[j, 1].wait_recv()
        relay(j)
    for j in (2, 3):
        b_copies[j, 0].wait_recv()
    group(2)
    for copy in relays:
        copy.wait_recv()
    group(3)

    for copy in list(a_copies.values()) + list(b_copies.values()) + relays:
        copy.wait_send()
    for g in range(4):
        some = pl.ds(0, 31)
        pltpu.make_async_copy(res.at[g, some], recv.at[g, some], c_send.at[g]).wait()
        pltpu.make_async_copy(res.at[g], recv.at[g], c_recv.at[g]).wait()


def finish_kernel(recv, out, mixed):
    z = lax.axis_index("acq") // 4
    low = lanes((8, 128)) < 64

    def arrange(x, y, m):
        def half_turn(v):
            return pltpu.roll(v.reshape(512, 128), 64, axis=1).reshape(v.shape)

        first = jnp.where(low, x, half_turn(y))
        second = jnp.where(low, half_turn(x), y)
        both = jnp.stack([first, second], axis=3)
        both = both.transpose(0, 2, 1, 3, 4, 5, 6)
        mixed[m] = both.reshape(1024, 128)

    parts = [recv[g].astype(F32).reshape(2, 4, 2, 4, 8, 128) for g in range(4)]
    arrange(parts[0], parts[3], 0)
    near = jnp.concatenate([parts[1][:, 0:2], parts[2][:, 2:4]], axis=1)
    far = jnp.concatenate([parts[2][:, 0:2], parts[1][:, 2:4]], axis=1)
    arrange(near, far, 1)
    for i in range(8):
        for m in range(2):
            y = mixed[m, pl.ds(i, 128, stride=8), :].T
            for n in range(8):
                if m == 0:
                    offset, t = (n // 4) * 2, n % 4
                else:
                    offset, t = 3 + (n // 2) % 2 * 2, (n // 4) * 2 + n % 2
                at = ((z + offset) % 4) * 32 + t * 8
                for part in range(2):
                    lane = n * 16 + part * 8
                    out[part, i, pl.ds(pl.multiple_of(at, 8), 8), :] = y[lane : lane + 8]


def local(scene_lines, assigned_area):
    smem = pl.BlockSpec(memory_space=pltpu.SMEM)
    vmem = pl.BlockSpec(memory_space=pltpu.VMEM)
    hbm = pl.BlockSpec(memory_space=pl.ANY)
    blocks = (4, 32, 4, 16, 128)
    got = pl.pallas_call(
        pairs_kernel,
        out_shape=jax.ShapeDtypeStruct(blocks, BF16),
        in_specs=[smem, vmem],
        out_specs=hbm,
        scratch_shapes=[
            pltpu.VMEM((4, 768, 128), F32),
            pltpu.VMEM((4, 48, 16, 128), BF16),
            pltpu.VMEM((2, 8, 128), jnp.int32),
            pltpu.SMEM((2, 8, 128), jnp.int32),
            pltpu.VMEM((48, 64, 128), BF16),
            pltpu.VMEM((48, 64, 128), BF16),
            pltpu.VMEM((48, 64, 128), BF16),
            pltpu.VMEM((48, 64, 128), BF16),
            pltpu.VMEM((16, 256, 512), BF16),
            pltpu.VMEM((16, 16, 8, 128), F32),
            pltpu.VMEM(blocks, BF16),
            pltpu.SemaphoreType.DMA((2,)),
            pltpu.SemaphoreType.DMA((4,)),
            pltpu.SemaphoreType.DMA((4,)),
            pltpu.SemaphoreType.DMA((12,)),
            pltpu.SemaphoreType.DMA((12,)),
            pltpu.SemaphoreType.DMA((4,)),
            pltpu.SemaphoreType.DMA((4,)),
        ],
        compiler_params=pltpu.CompilerParams(
            vmem_limit_bytes=40 << 20, collective_id=0, has_side_effects=True
        ),
    )(assigned_area, scene_lines)
    return pl.pallas_call(
        finish_kernel,
        grid=(4,),
        out_shape=jax.ShapeDtypeStruct((2, 8, 128, 512), F32),
        in_specs=[pl.BlockSpec((4, 8, 4, 16, 128), lambda n: (0, n, 0, 0, 0))],
        out_specs=pl.BlockSpec((2, 8, 128, 128), lambda n: (0, 0, 0, n)),
        scratch_shapes=[pltpu.VMEM((2, 1024, 128), F32)],
        compiler_params=pltpu.CompilerParams(vmem_limit_bytes=32 << 20),
    )(got)


def solution(mesh):
    placed = (P(None, "acq", "region", None), P("region", None))
    return jax.shard_map(
        local, mesh=mesh, in_specs=placed, out_specs=P(None, "acq", None, "region"), check_vma=False
    )
```

```python
import jax
import jax.numpy as jnp
import numpy as np
from jax import lax
from jax.experimental import pallas as pl
from jax.experimental.pallas import tpu as pltpu
from jax.sharding import PartitionSpec as P

F32 = jnp.float32
BF16 = jnp.bfloat16
NT = (((1,), (1,)), ((), ()))
MESH = pl.DeviceIdType.MESH


def taper(length, centre, width):
    index = np.arange(length, dtype=np.float32)
    values = np.exp(np.float32(-0.5) * ((index - np.float32(centre)) / np.float32(width)) ** 2)
    return values / np.sum(values)


ROWS = [float(v) for v in taper(4, 1.5, 1.5)]
COLS = [float(v) for v in taper(16, 7.5, 5.0).astype(jnp.bfloat16).astype(np.float32)]


def lanes(shape):
    return lax.broadcasted_iota(jnp.int32, shape, len(shape) - 1)


def column_weights():
    col = lanes((8, 128))
    values = jnp.zeros((8, 128), F32)
    for k in range(16):
        values = jnp.where(col % 16 == k, COLS[k], values)
    return values


def swap_parts(x):
    up = pltpu.roll(x, 120, axis=x.ndim - 1)
    down = pltpu.roll(x, 8, axis=x.ndim - 1)
    return jnp.where((lanes(x.shape) // 8) % 2 == 0, up, down)


def sort_rows(area, table):
    slot = lanes((8, 128))
    owner, place = slot // 8, slot % 8
    source = jnp.zeros((8, 128), jnp.int32)
    held = jnp.zeros((8, 128), jnp.int32)
    count = jnp.zeros((8, 128), jnp.int32)
    for b in range(48):
        hit = owner == area[0, b]
        take = jnp.logical_and(hit, count == place)
        source = jnp.where(take, b, source)
        held = jnp.where(take, 1, held)
        count = count + hit.astype(jnp.int32)
    table[0] = source
    table[1] = held


def stage_columns(lines, wide, staged):
    for n in range(16):
        wide[n * 48 : (n + 1) * 48, :] = lines[n // 8, n % 8].astype(F32)

    def row(b, _):
        staged[b] = wide[pl.ds(b, 16, stride=48), :].astype(BF16)
        return 0

    lax.fori_loop(0, 48, row, 0, unroll=8)


def build_own(w, src, weights, rows, at, lhs):
    look = (lanes((8, 128)) // 16) % 4
    for r in range(4):
        s = w * 4 + r
        table = weights * (ROWS[r] * src[1, 0, s].astype(F32))
        own = rows[src[0, 0, s]].astype(F32).reshape(2, 8, 128)
        spread = jnp.stack([own * jnp.where(look == l, table, 0.0)[None] for l in range(4)], axis=0)
        lhs[w, pl.ds(at, 64), r * 128 : (r + 1) * 128] = spread.reshape(64, 128).astype(BF16)


def window_sums(w, src, weights, z, lhs):
    zero = jnp.zeros((64, 128), BF16)
    low = lanes((64, 128)) < 64
    look = (lanes((8, 128)) // 16) % 4 == lax.broadcasted_iota(jnp.int32, (8, 128), 0)
    data, power, looks = [], [], []
    for r in range(4):
        s = w * 4 + r
        row = z[src[0, 0, s]]
        square = row * row
        data.append(jnp.concatenate([jnp.where(low, row, zero), jnp.where(low, zero, row)], axis=0))
        power.append(
            jnp.concatenate([jnp.where(low, square, zero), jnp.where(low, zero, square)], axis=0)
        )
        table = weights * (ROWS[r] * src[1, 0, s].astype(F32))
        looks.append(jnp.where(look, table, 0.0).astype(BF16))
    data = jnp.concatenate(data, axis=1)
    power = jnp.concatenate(power, axis=1)
    looks = jnp.concatenate(looks, axis=1)
    full = lax.dot_general(lhs[w], data, NT, preferred_element_type=F32)
    halves = lax.dot_general(looks, power, NT, preferred_element_type=F32)
    return full, halves + swap_parts(halves)


def own_intensities(w, intensity, own_power):
    turned = intensity.T
    low = lanes((8, 128)) < 64
    for q in range(4):
        for l in range(4):
            first = jnp.broadcast_to(turned[q * 16 : q * 16 + 8, l : l + 1], (8, 128))
            second = jnp.broadcast_to(turned[64 + q * 16 : 72 + q * 16, l : l + 1], (8, 128))
            own_power[w, q * 4 + l] = jnp.where(low, first, second)


def coherence(full, intensity, own):
    full = full.reshape(16, 2, 8, 128)
    sign = jnp.where((lanes((8, 128)) // 8) % 2 == 0, 1.0, -1.0).astype(F32)
    swapped = swap_parts(full[:, 1].reshape(128, 128)).reshape(16, 8, 128)
    total = swapped + sign[None] * full[:, 0]
    other = jnp.stack([jnp.broadcast_to(intensity[l : l + 1], (8, 128)) for l in range(4)], axis=0)
    product = own.reshape(4, 4, 8, 128) * other[None]
    scale = lax.rsqrt(product + 1e-6)
    return (total.reshape(4, 4, 8, 128) * scale).reshape(4, 2, 16, 128).astype(BF16)


def pairs_kernel(
    area, scene, recv,
    lines, wide, staged, mate, table, src, z0, z1, z2, z3, lhs, own_power, res,
    local_sem, read_sem, a_send, a_recv, b_send, b_recv, c_send, c_recv,
):
    zs = (z0, z1, z2, z3)
    k = lax.axis_index("region")
    acq = lax.axis_index("acq")
    z = acq // 4
    q = acq % 4
    xl, core = q // 2, q % 2
    right = (k, ((z + 1) % 4) * 4 + q)
    left = (k, ((z + 3) % 4) * 4 + q)

    def tile(j):
        return ((xl + j // 2) % 2) * 2 + (core + j % 2) % 2

    def rows16(start):
        return pl.ds(pl.multiple_of(start, 16), 16)

    reads = {}
    for j in (2, 3, 0, 1):
        columns = pl.ds(pl.multiple_of(tile(j) * 128, 128), 128)
        reads[j] = pltpu.make_async_copy(scene.at[:, :, :, columns], lines.at[j], read_sem.at[j])
        reads[j].start()
    barrier = pltpu.get_barrier_semaphore()
    for peer in (left, right):
        pl.semaphore_signal(barrier, inc=1, device_id=peer, device_id_type=MESH)

    def greet(n, _):
        o, p = n // 4, n % 4

        @pl.when(jnp.logical_or(o != k, p != q))
        def _():
            pl.semaphore_signal(barrier, inc=1, device_id=(o, z * 4 + p), device_id_type=MESH)

        return 0

    lax.fori_loop(0, 32, greet, 0)

    for j in (2, 3):
        reads[j].wait()
        stage_columns(lines.at[j], wide.at[j], staged.at[j])
    pl.semaphore_wait(barrier, 33)

    def remote(from_ref, to_ref, send, recv, peer):
        return pltpu.make_async_remote_copy(
            src_ref=from_ref, dst_ref=to_ref, send_sem=send, recv_sem=recv,
            device_id=peer, device_id_type=MESH,
        )

    a_copies = {}

    def exchange(n, j, land):
        peer = (k, z * 4 + tile(j))
        a_copies[n] = remote(staged.at[j], land, a_send.at[n], a_recv.at[n], peer)
        a_copies[n].start()

    here16 = z0.at[:, rows16(q * 16), :]
    exchange(2, 2, here16)
    exchange(3, 3, here16)
    for j in (0, 1):
        reads[j].wait()
        stage_columns(lines.at[j], wide.at[j], staged.at[j])

    def near(j, side):
        return zs[1 + j // 2].at[:, rows16(side * 32 + ((core + j) % 2) * 16), :]

    b_copies = {}

    def send_along(j):
        data = staged.at[0] if j == 0 else zs[0].at[:, rows16(tile(j) * 16), :]
        for side, peer in ((0, right), (1, left)):
            n = side * 4 + j
            b_copies[j, side] = remote(data, near(j, side), b_send.at[n], b_recv.at[n], peer)
            b_copies[j, side].start()

    send_along(0)
    exchange(1, 1, here16)
    exchange(0, 1, mate)
    own = pltpu.make_async_copy(staged.at[0], here16, local_sem.at[1])
    own.start()
    sort_rows(area, table)
    sorted_rows = pltpu.make_async_copy(table, src, local_sem.at[0])
    sorted_rows.start()
    a_copies[1].wait_recv()
    send_along(1)
    a_copies[0].wait_recv()
    sorted_rows.wait()

    weights = column_weights()
    q64 = [pl.multiple_of(tile(j) * 64, 64) for j in range(4)]

    def build_near(w, _):
        build_own(w, src, weights, staged.at[0], q64[0], lhs)
        build_own(w, src, weights, mate, q64[1], lhs)
        return 0

    lax.fori_loop(0, 16, build_near, 0, unroll=2)
    for j in (2, 3):
        a_copies[j].wait_recv()
        send_along(j)
    own.wait()

    def send_results(o, g):
        for j in (2, 3, 1, 0):
            p = tile(j)
            block, land = res.at[g, o * 4 + p], recv.at[g, k * 4 + q]
            away = remote(block, land, c_send.at[g], c_recv.at[g], (o, z * 4 + p))
            if j:
                away.start()
                continue

            @pl.when(o == k)
            def _():
                pltpu.make_async_copy(block, land, c_recv.at[g]).start()

            @pl.when(o != k)
            def _():
                away.start()

    def z0_tile(j):
        return z0.at[:, rows16(tile(j) * 16), :]

    def distant(n, u):
        x = (1 - (n // 2) * (1 - n // 3)) if u == 0 else (n % 2) * (1 - n // 3)
        y = 2 - (n + 1) // 2 if u == 0 else 2 + (n + 1) // 2
        return ((k // 4 + x) % 2) * 4 + (k + y) % 4

    def group(g):
        def windows(regions):
            pairs = [(o, o * 2 + h) for o in regions for h in range(2)]
            if g == 0:
                for _, w in pairs:
                    for j in (2, 3):
                        build_own(w, src, weights, z0_tile(j), q64[j], lhs)
            sums = [window_sums(w, src, weights, zs[g], lhs) for _, w in pairs]
            if g == 0:
                for (_, w), (_, intensity) in zip(pairs, sums):
                    own_intensities(w, intensity, own_power)
            for n, ((o, w), (full, intensity)) in enumerate(zip(pairs, sums)):
                h = n % 2
                block = coherence(full, intensity, own_power[w])
                res[g, pl.ds(o * 4, 4), h * 2 : h * 2 + 2] = block
                if h:
                    send_results(o, g)

        def step(n, _):
            if g == 0:
                windows([distant(n, 0)])
                windows([distant(n, 1)])
            else:
                windows([distant(n, 0), distant(n, 1)])
            return 0

        lax.fori_loop(0, 4, step, 0)

    group(0)
    for j in (0, 1):
        for side in range(2):
            b_copies[j, side].wait_recv()
    group(1)

    relays = []

    def relay(j):
        side, peer = ((0, right), (0, right), (1, left), (1, left))[j]
        n = 8 + j
        relays.append(remote(
            near(j, side), zs[3].at[:, rows16(tile(j) * 16), :], b_send.at[n], b_recv.at[n], peer
        ))
        relays[-1].start()

    for j in (2, 3):
        b_copies[j, 0].wait_recv()
        b_copies[j, 1].wait_recv()
        relay(j - 2)
        relay(j)
    group(2)
    for copy in relays:
        copy.wait_recv()
    group(3)

    for copy in list(a_copies.values()) + list(b_copies.values()) + relays:
        copy.wait_send()
    for g in range(4):
        some = pl.ds(0, 31)
        pltpu.make_async_copy(res.at[g, some], recv.at[g, some], c_send.at[g]).wait()
        pltpu.make_async_copy(res.at[g], recv.at[g], c_recv.at[g]).wait()


def finish_kernel(recv, out, got, built, mixed, read_sem, write_sem):
    z = lax.axis_index("acq") // 4
    low = lanes((8, 128)) < 64
    reads = []
    for n in range(4):
        some = pl.ds(n * 8, 8)
        reads.append(pltpu.make_async_copy(recv.at[:, some], got.at[n], read_sem.at[n]))
        reads[-1].start()

    def arrange(x, y, m):
        def half_turn(v):
            return pltpu.roll(v.reshape(512, 128), 64, axis=1).reshape(v.shape)

        first = jnp.where(low, x, half_turn(y))
        second = jnp.where(low, half_turn(x), y)
        both = jnp.stack([first, second], axis=3)
        both = both.transpose(0, 2, 1, 3, 4, 5, 6)
        mixed[m] = both.reshape(1024, 128)

    writes = []
    for n in range(4):
        reads[n].wait()
        parts = [got[n, g].astype(F32).reshape(2, 4, 2, 4, 8, 128) for g in range(4)]
        arrange(parts[0], parts[3], 0)
        near = jnp.concatenate([parts[1][:, 0:2], parts[2][:, 2:4]], axis=1)
        far = jnp.concatenate([parts[2][:, 0:2], parts[1][:, 2:4]], axis=1)
        arrange(near, far, 1)
        for i in range(8):
            for m in range(2):
                y = mixed[m, pl.ds(i, 128, stride=8), :].T
                for t in range(8):
                    if m == 0:
                        offset, tile = (t // 4) * 2, t % 4
                    else:
                        offset, tile = 3 + (t // 2) % 2 * 2, (t // 4) * 2 + t % 2
                    at = pl.multiple_of(((z + offset) % 4) * 32 + tile * 8, 8)
                    for part in range(2):
                        lane = t * 16 + part * 8
                        built[n, part, i, pl.ds(at, 8), :] = y[lane : lane + 8]
        columns = pl.ds(n * 128, 128)
        writes.append(
            pltpu.make_async_copy(built.at[n], out.at[:, :, :, columns], write_sem.at[n])
        )
        writes[-1].start()
    for write in writes:
        write.wait()


def local(scene_lines, assigned_area):
    smem = pl.BlockSpec(memory_space=pltpu.SMEM)
    hbm = pl.BlockSpec(memory_space=pltpu.HBM)
    blocks = (4, 32, 4, 16, 128)
    got = pl.pallas_call(
        pairs_kernel,
        out_shape=jax.ShapeDtypeStruct(blocks, BF16),
        in_specs=[smem, hbm],
        out_specs=hbm,
        scratch_shapes=[
            pltpu.VMEM((4, 2, 8, 48, 128), BF16),
            pltpu.VMEM((4, 768, 128), F32),
            pltpu.VMEM((4, 48, 16, 128), BF16),
            pltpu.VMEM((48, 16, 128), BF16),
            pltpu.VMEM((2, 8, 128), jnp.int32),
            pltpu.SMEM((2, 8, 128), jnp.int32),
            pltpu.VMEM((48, 64, 128), BF16),
            pltpu.VMEM((48, 64, 128), BF16),
            pltpu.VMEM((48, 64, 128), BF16),
            pltpu.VMEM((48, 64, 128), BF16),
            pltpu.VMEM((16, 256, 512), BF16),
            pltpu.VMEM((16, 16, 8, 128), F32),
            pltpu.VMEM(blocks, BF16),
            pltpu.SemaphoreType.DMA((2,)),
            pltpu.SemaphoreType.DMA((4,)),
            pltpu.SemaphoreType.DMA((4,)),
            pltpu.SemaphoreType.DMA((4,)),
            pltpu.SemaphoreType.DMA((12,)),
            pltpu.SemaphoreType.DMA((12,)),
            pltpu.SemaphoreType.DMA((4,)),
            pltpu.SemaphoreType.DMA((4,)),
        ],
        compiler_params=pltpu.CompilerParams(
            vmem_limit_bytes=61 << 20, collective_id=0, has_side_effects=True
        ),
    )(assigned_area.reshape(1, 48), scene_lines)
    return pl.pallas_call(
        finish_kernel,
        out_shape=jax.ShapeDtypeStruct((2, 8, 128, 512), F32),
        in_specs=[pl.BlockSpec(memory_space=pltpu.HBM)],
        out_specs=pl.BlockSpec(memory_space=pltpu.HBM),
        scratch_shapes=[
            pltpu.VMEM((4, 4, 8, 4, 16, 128), BF16),
            pltpu.VMEM((4, 2, 8, 128, 128), F32),
            pltpu.VMEM((2, 1024, 128), F32),
            pltpu.SemaphoreType.DMA((4,)),
            pltpu.SemaphoreType.DMA((4,)),
        ],
        compiler_params=pltpu.CompilerParams(vmem_limit_bytes=61 << 20),
    )(got)


def solution(mesh):
    placed = (P(None, "acq", "region", None), P("region", None))
    return jax.shard_map(
        local, mesh=mesh, in_specs=placed, out_specs=P(None, "acq", None, "region"), check_vma=False
    )
```

```python
import jax
import jax.numpy as jnp
import numpy as np
from jax import lax
from jax.experimental import pallas as pl
from jax.experimental.pallas import tpu as pltpu
from jax.sharding import PartitionSpec as P

F32 = jnp.float32
BF16 = jnp.bfloat16
NT = (((1,), (1,)), ((), ()))
MESH = pl.DeviceIdType.MESH


def taper(length, centre, width):
    index = np.arange(length, dtype=np.float32)
    values = np.exp(np.float32(-0.5) * ((index - np.float32(centre)) / np.float32(width)) ** 2)
    return values / np.sum(values)


ROWS = [float(v) for v in taper(4, 1.5, 1.5)]
COLS = [float(v) for v in taper(16, 7.5, 5.0).astype(jnp.bfloat16).astype(np.float32)]


def lanes(shape):
    return lax.broadcasted_iota(jnp.int32, shape, len(shape) - 1)


def column_weights():
    col = lanes((8, 128))
    values = jnp.zeros((8, 128), F32)
    for k in range(16):
        values = jnp.where(col % 16 == k, COLS[k], values)
    return values


def swap_parts(x):
    up = pltpu.roll(x, 120, axis=x.ndim - 1)
    down = pltpu.roll(x, 8, axis=x.ndim - 1)
    return jnp.where((lanes(x.shape) // 8) % 2 == 0, up, down)


def sort_rows(area, table):
    slot = lanes((8, 128))
    owner, place = slot // 8, slot % 8
    source = jnp.zeros((8, 128), jnp.int32)
    held = jnp.zeros((8, 128), jnp.int32)
    count = jnp.zeros((8, 128), jnp.int32)
    for b in range(48):
        hit = owner == area[0, b]
        take = jnp.logical_and(hit, count == place)
        source = jnp.where(take, b, source)
        held = jnp.where(take, 1, held)
        count = count + hit.astype(jnp.int32)
    table[0] = source
    table[1] = held


def stage_columns(lines, wide, staged):
    for n in range(16):
        wide[n * 48 : (n + 1) * 48, :] = lines[n // 8, n % 8].astype(F32)

    def row(b, _):
        staged[b] = wide[pl.ds(b, 16, stride=48), :].astype(BF16)
        return 0

    lax.fori_loop(0, 48, row, 0, unroll=8)


def build_own(w, src, weights, rows, at, lhs):
    look = (lanes((8, 128)) // 16) % 4
    for r in range(4):
        s = w * 4 + r
        table = weights * (ROWS[r] * src[1, 0, s].astype(F32))
        own = rows[src[0, 0, s]].astype(F32).reshape(2, 8, 128)
        spread = jnp.stack([own * jnp.where(look == l, table, 0.0)[None] for l in range(4)], axis=0)
        lhs[w, pl.ds(at, 64), r * 128 : (r + 1) * 128] = spread.reshape(64, 128).astype(BF16)


def window_sums(w, src, weights, z, lhs):
    zero = jnp.zeros((64, 128), BF16)
    low = lanes((64, 128)) < 64
    look = (lanes((8, 128)) // 16) % 4 == lax.broadcasted_iota(jnp.int32, (8, 128), 0)
    data, power, looks = [], [], []
    for r in range(4):
        s = w * 4 + r
        row = z[src[0, 0, s]]
        square = row * row
        data.append(jnp.concatenate([jnp.where(low, row, zero), jnp.where(low, zero, row)], axis=0))
        power.append(
            jnp.concatenate([jnp.where(low, square, zero), jnp.where(low, zero, square)], axis=0)
        )
        table = weights * (ROWS[r] * src[1, 0, s].astype(F32))
        looks.append(jnp.where(look, table, 0.0).astype(BF16))
    data = jnp.concatenate(data, axis=1)
    power = jnp.concatenate(power, axis=1)
    looks = jnp.concatenate(looks, axis=1)
    full = lax.dot_general(lhs[w], data, NT, preferred_element_type=F32)
    halves = lax.dot_general(looks, power, NT, preferred_element_type=F32)
    return full, halves + swap_parts(halves)


def own_intensities(w, intensity, own_power):
    turned = intensity.T
    low = lanes((8, 128)) < 64
    for q in range(4):
        for l in range(4):
            first = jnp.broadcast_to(turned[q * 16 : q * 16 + 8, l : l + 1], (8, 128))
            second = jnp.broadcast_to(turned[64 + q * 16 : 72 + q * 16, l : l + 1], (8, 128))
            own_power[w, q * 4 + l] = jnp.where(low, first, second)


def coherence(full, intensity, own):
    full = full.reshape(16, 2, 8, 128)
    sign = jnp.where((lanes((8, 128)) // 8) % 2 == 0, 1.0, -1.0).astype(F32)
    swapped = swap_parts(full[:, 1].reshape(128, 128)).reshape(16, 8, 128)
    total = swapped + sign[None] * full[:, 0]
    other = jnp.stack([jnp.broadcast_to(intensity[l : l + 1], (8, 128)) for l in range(4)], axis=0)
    product = own.reshape(4, 4, 8, 128) * other[None]
    scale = lax.rsqrt(product + 1e-6)
    return (total.reshape(4, 4, 8, 128) * scale).reshape(4, 2, 16, 128).astype(BF16)


def side_by_side(x, y, mixed):
    low = lanes((8, 128)) < 64

    def half_turn(v):
        return pltpu.roll(v.reshape(512, 128), 64, axis=1).reshape(v.shape)

    first = jnp.where(low, x, half_turn(y))
    second = jnp.where(low, half_turn(x), y)
    both = jnp.stack([first, second], axis=3)
    both = both.transpose(0, 2, 1, 3, 4, 5, 6)
    mixed[...] = both.reshape(1024, 128)


def blocks_of(x):
    return x.astype(F32).reshape(2, 4, 2, 4, 8, 128)


def pairs_kernel(
    area, scene, recv, turned,
    lines, wide, staged, mate, table, src, z0, z1, z2, z3, lhs, own_power, res, landed, mixed, built,
    turn_sem, local_sem, read_sem, a_send, a_recv, b_send, b_recv, c_send, c_recv,
):
    zs = (z0, z1, z2, z3)
    lands = (recv.at[0], landed.at[0], landed.at[1], recv.at[1])
    k = lax.axis_index("region")
    acq = lax.axis_index("acq")
    z = acq // 4
    q = acq % 4
    xl, core = q // 2, q % 2
    right = (k, ((z + 1) % 4) * 4 + q)
    left = (k, ((z + 3) % 4) * 4 + q)

    def tile(j):
        return ((xl + j // 2) % 2) * 2 + (core + j % 2) % 2

    def rows16(start):
        return pl.ds(pl.multiple_of(start, 16), 16)

    reads = {}
    for j in (2, 3, 0, 1):
        columns = pl.ds(pl.multiple_of(tile(j) * 128, 128), 128)
        reads[j] = pltpu.make_async_copy(scene.at[:, :, :, columns], lines.at[j], read_sem.at[j])
        reads[j].start()
    barrier = pltpu.get_barrier_semaphore()
    for peer in (left, right):
        pl.semaphore_signal(barrier, inc=1, device_id=peer, device_id_type=MESH)

    def greet(n, _):
        o, p = n // 4, n % 4

        @pl.when(jnp.logical_or(o != k, p != q))
        def _():
            pl.semaphore_signal(barrier, inc=1, device_id=(o, z * 4 + p), device_id_type=MESH)

        return 0

    lax.fori_loop(0, 32, greet, 0)

    for j in (2, 3):
        reads[j].wait()
        stage_columns(lines.at[j], wide.at[j], staged.at[j])
    pl.semaphore_wait(barrier, 33)

    def remote(from_ref, to_ref, send, recv, peer):
        return pltpu.make_async_remote_copy(
            src_ref=from_ref, dst_ref=to_ref, send_sem=send, recv_sem=recv,
            device_id=peer, device_id_type=MESH,
        )

    a_copies = {}

    def exchange(n, j, land):
        peer = (k, z * 4 + tile(j))
        a_copies[n] = remote(staged.at[j], land, a_send.at[n], a_recv.at[n], peer)
        a_copies[n].start()

    here16 = z0.at[:, rows16(q * 16), :]
    exchange(2, 2, here16)
    exchange(3, 3, here16)
    for j in (0, 1):
        reads[j].wait()
        stage_columns(lines.at[j], wide.at[j], staged.at[j])

    def near(j, side):
        return zs[1 + j // 2].at[:, rows16(side * 32 + ((core + j) % 2) * 16), :]

    b_copies = {}

    def send_along(j):
        data = staged.at[0] if j == 0 else zs[0].at[:, rows16(tile(j) * 16), :]
        for side, peer in ((0, right), (1, left)):
            n = side * 4 + j
            b_copies[j, side] = remote(data, near(j, side), b_send.at[n], b_recv.at[n], peer)
            b_copies[j, side].start()

    send_along(0)
    exchange(1, 1, here16)
    exchange(0, 1, mate)
    own = pltpu.make_async_copy(staged.at[0], here16, local_sem.at[1])
    own.start()
    sort_rows(area, table)
    sorted_rows = pltpu.make_async_copy(table, src, local_sem.at[0])
    sorted_rows.start()
    a_copies[1].wait_recv()
    send_along(1)
    a_copies[0].wait_recv()
    sorted_rows.wait()

    weights = column_weights()
    q64 = [pl.multiple_of(tile(j) * 64, 64) for j in range(4)]

    def build_near(w, _):
        build_own(w, src, weights, staged.at[0], q64[0], lhs)
        build_own(w, src, weights, mate, q64[1], lhs)
        return 0

    lax.fori_loop(0, 16, build_near, 0, unroll=2)
    for j in (2, 3):
        a_copies[j].wait_recv()
        send_along(j)
    own.wait()

    def send_results(o, g):
        for j in (2, 3, 1, 0):
            p = tile(j)
            block, land = res.at[g, o * 4 + p], lands[g].at[k * 4 + q]
            away = remote(block, land, c_send.at[g], c_recv.at[g], (o, z * 4 + p))
            if j:
                away.start()
                continue

            @pl.when(o == k)
            def _():
                pltpu.make_async_copy(block, land, c_recv.at[g]).start()

            @pl.when(o != k)
            def _():
                away.start()

    def z0_tile(j):
        return z0.at[:, rows16(tile(j) * 16), :]

    def distant(n, u):
        x = (1 - (n // 2) * (1 - n // 3)) if u == 0 else (n % 2) * (1 - n // 3)
        y = 2 - (n + 1) // 2 if u == 0 else 2 + (n + 1) // 2
        return ((k // 4 + x) % 2) * 4 + (k + y) % 4

    def group(g):
        def windows(regions):
            pairs = [(o, o * 2 + h) for o in regions for h in range(2)]
            if g == 0:
                for _, w in pairs:
                    for j in (2, 3):
                        build_own(w, src, weights, z0_tile(j), q64[j], lhs)
            sums = [window_sums(w, src, weights, zs[g], lhs) for _, w in pairs]
            if g == 0:
                for (_, w), (_, intensity) in zip(pairs, sums):
                    own_intensities(w, intensity, own_power)
            for n, ((o, w), (full, intensity)) in enumerate(zip(pairs, sums)):
                h = n % 2
                block = coherence(full, intensity, own_power[w])
                res[g, pl.ds(o * 4, 4), h * 2 : h * 2 + 2] = block
                if h:
                    send_results(o, g)

        def step(n, _):
            windows([distant(n, 0), distant(n, 1)])
            return 0

        lax.fori_loop(0, 4, step, 0)

    group(0)
    for j in (0, 1):
        for side in range(2):
            b_copies[j, side].wait_recv()
    group(1)

    relays = []

    def relay(j):
        side, peer = ((0, right), (0, right), (1, left), (1, left))[j]
        n = 8 + j
        relays.append(remote(
            near(j, side), zs[3].at[:, rows16(tile(j) * 16), :], b_send.at[n], b_recv.at[n], peer
        ))
        relays[-1].start()

    for j in (2, 3):
        b_copies[j, 0].wait_recv()
        b_copies[j, 1].wait_recv()
        relay(j - 2)
        relay(j)
    group(2)
    for copy in relays:
        copy.wait_recv()
    group(3)

    for g in (1, 2):
        pltpu.make_async_copy(res.at[g], lands[g], c_recv.at[g]).wait()

    def turn(n, _):
        same = blocks_of(landed[0, pl.ds(n * 8, 8)])
        cross = blocks_of(landed[1, pl.ds(n * 8, 8)])
        near = jnp.concatenate([same[:, 0:2], cross[:, 2:4]], axis=1)
        far = jnp.concatenate([cross[:, 0:2], same[:, 2:4]], axis=1)
        side_by_side(near, far, mixed)
        for i in range(8):
            y = mixed[pl.ds(i, 128, stride=8), :].T
            for x in range(2):
                for side in range(2):
                    for part in range(2):
                        lane = x * 64 + side * 32 + part * 8
                        pair = jnp.concatenate([y[lane : lane + 8], y[lane + 16 : lane + 24]], axis=0)
                        built[n, part, i, side, x * 16 : x * 16 + 16, :] = pair.astype(BF16)
        columns = pl.ds(pl.multiple_of(n * 128, 128), 128)
        pltpu.make_async_copy(
            built.at[n], turned.at[:, :, :, :, columns], turn_sem.at[n]
        ).start()
        return 0

    lax.fori_loop(0, 4, turn, 0)

    for copy in list(a_copies.values()) + list(b_copies.values()) + relays:
        copy.wait_send()
    for n in range(4):
        columns = pl.ds(n * 128, 128)
        pltpu.make_async_copy(
            built.at[n], turned.at[:, :, :, :, columns], turn_sem.at[n]
        ).wait()
    for g in range(4):
        some = pl.ds(0, 31)
        pltpu.make_async_copy(res.at[g, some], lands[g].at[some], c_send.at[g]).wait()
    for g in (0, 3):
        pltpu.make_async_copy(res.at[g], lands[g], c_recv.at[g]).wait()


def finish_kernel(recv, turned, out, wide, built, mixed, write_sem, wide_sem):
    z = lax.axis_index("acq") // 4

    def rows_of(offset):
        return pl.ds(pl.multiple_of(((z + offset) % 4) * 32, 32), 32)

    copies = []

    def write(from_ref, to_ref, sem):
        copies.append(pltpu.make_async_copy(from_ref, to_ref, sem))
        copies[-1].start()

    for part in range(2):
        wide[part] = turned[part].astype(F32)
        for d in range(2):
            land = out.at[part, :, rows_of(3 + 2 * d)]
            write(wide.at[part, :, d], land, wide_sem.at[part, d])
    for n in range(4):
        some = slice(n * 8, n * 8 + 8)
        side_by_side(blocks_of(recv[0, some]), blocks_of(recv[1, some]), mixed)
        for i in range(8):
            y = mixed[pl.ds(i, 128, stride=8), :].T
            for t in range(8):
                for part in range(2):
                    lane, at = t * 16 + part * 8, (t % 4) * 8
                    built[n, t // 4, part, i, at : at + 8, :] = y[lane : lane + 8]
        columns = pl.ds(n * 128, 128)
        for d in range(2):
            write(built.at[n, d], out.at[:, :, rows_of(2 * d), columns], write_sem.at[n, d])
    for copy in copies:
        copy.wait()


def local(scene_lines, assigned_area):
    smem = pl.BlockSpec(memory_space=pltpu.SMEM)
    vmem = pl.BlockSpec(memory_space=pltpu.VMEM)
    hbm = pl.BlockSpec(memory_space=pltpu.HBM)
    blocks = (4, 32, 4, 16, 128)
    got = pl.pallas_call(
        pairs_kernel,
        out_shape=[
            jax.ShapeDtypeStruct((2, 32, 4, 16, 128), BF16),
            jax.ShapeDtypeStruct((2, 8, 2, 32, 512), BF16),
        ],
        in_specs=[smem, hbm],
        out_specs=[hbm, hbm],
        scratch_shapes=[
            pltpu.VMEM((4, 2, 8, 48, 128), BF16),
            pltpu.VMEM((4, 768, 128), F32),
            pltpu.VMEM((4, 48, 16, 128), BF16),
            pltpu.VMEM((48, 16, 128), BF16),
            pltpu.VMEM((2, 8, 128), jnp.int32),
            pltpu.SMEM((2, 8, 128), jnp.int32),
            pltpu.VMEM((48, 64, 128), BF16),
            pltpu.VMEM((48, 64, 128), BF16),
            pltpu.VMEM((48, 64, 128), BF16),
            pltpu.VMEM((48, 64, 128), BF16),
            pltpu.VMEM((16, 256, 512), BF16),
            pltpu.VMEM((16, 16, 8, 128), F32),
            pltpu.VMEM(blocks, BF16),
            pltpu.VMEM((2, 32, 4, 16, 128), BF16),
            pltpu.VMEM((1024, 128), F32),
            pltpu.VMEM((4, 2, 8, 2, 32, 128), BF16),
            pltpu.SemaphoreType.DMA((4,)),
            pltpu.SemaphoreType.DMA((2,)),
            pltpu.SemaphoreType.DMA((4,)),
            pltpu.SemaphoreType.DMA((4,)),
            pltpu.SemaphoreType.DMA((4,)),
            pltpu.SemaphoreType.DMA((12,)),
            pltpu.SemaphoreType.DMA((12,)),
            pltpu.SemaphoreType.DMA((4,)),
            pltpu.SemaphoreType.DMA((4,)),
        ],
        compiler_params=pltpu.CompilerParams(
            vmem_limit_bytes=40 << 20, collective_id=0, has_side_effects=True
        ),
    )(
        pltpu.with_memory_space_constraint(assigned_area.reshape(1, 48), pltpu.HBM),
        pltpu.with_memory_space_constraint(scene_lines, pltpu.HBM),
    )
    return pl.pallas_call(
        finish_kernel,
        out_shape=jax.ShapeDtypeStruct((2, 8, 128, 512), F32),
        in_specs=[vmem, vmem],
        out_specs=hbm,
        scratch_shapes=[
            pltpu.VMEM((2, 8, 2, 32, 512), F32),
            pltpu.VMEM((4, 2, 2, 8, 32, 128), F32),
            pltpu.VMEM((1024, 128), F32),
            pltpu.SemaphoreType.DMA((4, 2)),
            pltpu.SemaphoreType.DMA((2, 2)),
        ],
        compiler_params=pltpu.CompilerParams(vmem_limit_bytes=32 << 20),
    )(*got)


def solution(mesh):
    placed = (P(None, "acq", "region", None), P("region", None))
    return jax.shard_map(
        local, mesh=mesh, in_specs=placed, out_specs=P(None, "acq", None, "region"), check_vma=False
    )
```

```python
import jax
import jax.numpy as jnp
import numpy as np
from jax import lax
from jax.experimental import pallas as pl
from jax.experimental.pallas import tpu as pltpu
from jax.sharding import PartitionSpec as P

F32 = jnp.float32
BF16 = jnp.bfloat16
NT = (((1,), (1,)), ((), ()))
MESH = pl.DeviceIdType.MESH


def taper(length, centre, width):
    index = np.arange(length, dtype=np.float32)
    values = np.exp(np.float32(-0.5) * ((index - np.float32(centre)) / np.float32(width)) ** 2)
    return values / np.sum(values)


ROWS = [float(v) for v in taper(4, 1.5, 1.5)]
COLS = [float(v) for v in taper(16, 7.5, 5.0).astype(jnp.bfloat16).astype(np.float32)]


def lanes(shape):
    return lax.broadcasted_iota(jnp.int32, shape, len(shape) - 1)


def column_weights():
    col = lanes((8, 128))
    values = jnp.zeros((8, 128), F32)
    for k in range(16):
        values = jnp.where(col % 16 == k, COLS[k], values)
    return values


def swap_parts(x):
    up = pltpu.roll(x, 120, axis=x.ndim - 1)
    down = pltpu.roll(x, 8, axis=x.ndim - 1)
    return jnp.where((lanes(x.shape) // 8) % 2 == 0, up, down)


def sort_rows(area, table):
    slot = lanes((8, 128))
    owner, place = slot // 8, slot % 8
    source = jnp.zeros((8, 128), jnp.int32)
    held = jnp.zeros((8, 128), jnp.int32)
    count = jnp.zeros((8, 128), jnp.int32)
    for b in range(48):
        hit = owner == area[0, b]
        take = jnp.logical_and(hit, count == place)
        source = jnp.where(take, b, source)
        held = jnp.where(take, 1, held)
        count = count + hit.astype(jnp.int32)
    table[0] = source
    table[1] = held


def stage_columns(lines, wide, staged):
    for n in range(16):
        wide[n * 48 : (n + 1) * 48, :] = lines[n // 8, n % 8].astype(F32)

    def row(b, _):
        staged[b] = wide[pl.ds(b, 16, stride=48), :].astype(BF16)
        return 0

    lax.fori_loop(0, 48, row, 0, unroll=8)


def build_own(w, src, weights, rows, at, lhs):
    look = (lanes((8, 128)) // 16) % 4
    for r in range(4):
        s = w * 4 + r
        table = weights * (ROWS[r] * src[1, 0, s].astype(F32))
        own = rows[src[0, 0, s]].astype(F32).reshape(2, 8, 128)
        spread = jnp.stack([own * jnp.where(look == l, table, 0.0)[None] for l in range(4)], axis=0)
        lhs[w, pl.ds(at, 64), r * 128 : (r + 1) * 128] = spread.reshape(64, 128).astype(BF16)


def window_sums(w, src, weights, z, lhs):
    zero = jnp.zeros((64, 128), BF16)
    low = lanes((64, 128)) < 64
    look = (lanes((8, 128)) // 16) % 4 == lax.broadcasted_iota(jnp.int32, (8, 128), 0)
    data, power, looks = [], [], []
    for r in range(4):
        s = w * 4 + r
        row = z[src[0, 0, s]]
        square = row * row
        data.append(jnp.concatenate([jnp.where(low, row, zero), jnp.where(low, zero, row)], axis=0))
        power.append(
            jnp.concatenate([jnp.where(low, square, zero), jnp.where(low, zero, square)], axis=0)
        )
        table = weights * (ROWS[r] * src[1, 0, s].astype(F32))
        looks.append(jnp.where(look, table, 0.0).astype(BF16))
    data = jnp.concatenate(data, axis=1)
    power = jnp.concatenate(power, axis=1)
    looks = jnp.concatenate(looks, axis=1)
    full = lax.dot_general(lhs[w], data, NT, preferred_element_type=F32)
    halves = lax.dot_general(looks, power, NT, preferred_element_type=F32)
    return full, halves + swap_parts(halves)


def own_intensities(w, intensity, own_power):
    lane = lanes((8, 128))
    same = lane % 16 == lax.broadcasted_iota(jnp.int32, (8, 128), 0)
    picked = []
    for q in range(4):
        mine = jnp.logical_and(same, (lane // 16) % 4 == q)
        for l in range(4):
            row = jnp.broadcast_to(intensity[l : l + 1], (8, 128))
            picked.append(jnp.where(mine, row, 0.0))
    picked = jnp.concatenate(picked, axis=0)
    coarse = picked.astype(BF16)
    fine = (picked - coarse.astype(F32)).astype(BF16)
    terms = jnp.concatenate([coarse, fine], axis=1)
    lane = lanes((128, 256)) % 128
    half = lax.broadcasted_iota(jnp.int32, (128, 256), 0)
    spread = jnp.where((lane < 64) == (half < 64), 1.0, 0.0).astype(BF16)
    both = lax.dot_general(terms, spread, NT, preferred_element_type=F32)
    own_power[w] = both.reshape(16, 8, 128)


def coherence(full, intensity, own):
    full = full.reshape(16, 2, 8, 128)
    sign = jnp.where((lanes((8, 128)) // 8) % 2 == 0, 1.0, -1.0).astype(F32)
    swapped = swap_parts(full[:, 1].reshape(128, 128)).reshape(16, 8, 128)
    total = swapped + sign[None] * full[:, 0]
    other = jnp.stack([jnp.broadcast_to(intensity[l : l + 1], (8, 128)) for l in range(4)], axis=0)
    product = own.reshape(4, 4, 8, 128) * other[None]
    scale = lax.rsqrt(product + 1e-6)
    return (total.reshape(4, 4, 8, 128) * scale).reshape(4, 2, 16, 128).astype(BF16)


def side_by_side(x, y, mixed):
    low = lanes((8, 128)) < 64

    def half_turn(v):
        return pltpu.roll(v.reshape(512, 128), 64, axis=1).reshape(v.shape)

    first = jnp.where(low, x, half_turn(y))
    second = jnp.where(low, half_turn(x), y)
    both = jnp.stack([first, second], axis=3)
    both = both.transpose(0, 2, 1, 3, 4, 5, 6)
    mixed[...] = both.reshape(1024, 128)


def blocks_of(x):
    return x.astype(F32).reshape(2, 4, 2, 4, 8, 128)


def pairs_kernel(
    area, scene, recv, turned,
    lines, wide, staged, mate, table, src, z0, z1, z2, z3, lhs, own_power, res, landed, mixed, built,
    turn_sem, local_sem, read_sem, a_send, a_recv, b_send, b_recv, c_send, c_recv,
):
    zs = (z0, z1, z2, z3)
    lands = (recv.at[0], landed.at[0], landed.at[1], recv.at[1])
    k = lax.axis_index("region")
    acq = lax.axis_index("acq")
    z = acq // 4
    q = acq % 4
    xl, core = q // 2, q % 2
    right = (k, ((z + 1) % 4) * 4 + q)
    left = (k, ((z + 3) % 4) * 4 + q)

    def tile(j):
        return ((xl + j // 2) % 2) * 2 + (core + j % 2) % 2

    def rows16(start):
        return pl.ds(pl.multiple_of(start, 16), 16)

    reads = {}
    for j in (2, 3, 0, 1):
        columns = pl.ds(pl.multiple_of(tile(j) * 128, 128), 128)
        reads[j] = pltpu.make_async_copy(scene.at[:, :, :, columns], lines.at[j], read_sem.at[j])
        reads[j].start()
    barrier = pltpu.get_barrier_semaphore()
    for peer in (left, right):
        pl.semaphore_signal(barrier, inc=1, device_id=peer, device_id_type=MESH)

    def greet(n, _):
        o, p = n // 4, n % 4

        @pl.when(jnp.logical_or(o != k, p != q))
        def _():
            pl.semaphore_signal(barrier, inc=1, device_id=(o, z * 4 + p), device_id_type=MESH)

        return 0

    lax.fori_loop(0, 32, greet, 0)

    for j in (2, 3):
        reads[j].wait()
        stage_columns(lines.at[j], wide.at[j], staged.at[j])
    pl.semaphore_wait(barrier, 33)

    def remote(from_ref, to_ref, send, recv, peer):
        return pltpu.make_async_remote_copy(
            src_ref=from_ref, dst_ref=to_ref, send_sem=send, recv_sem=recv,
            device_id=peer, device_id_type=MESH,
        )

    a_copies = {}

    def exchange(n, j, land):
        peer = (k, z * 4 + tile(j))
        a_copies[n] = remote(staged.at[j], land, a_send.at[n], a_recv.at[n], peer)
        a_copies[n].start()

    here16 = z0.at[:, rows16(q * 16), :]
    exchange(2, 2, here16)
    exchange(3, 3, here16)
    for j in (0, 1):
        reads[j].wait()
        stage_columns(lines.at[j], wide.at[j], staged.at[j])

    def near(j, side):
        return zs[1 + j // 2].at[:, rows16(side * 32 + ((core + j) % 2) * 16), :]

    b_copies = {}

    def send_along(j):
        data = staged.at[0] if j == 0 else zs[0].at[:, rows16(tile(j) * 16), :]
        for side, peer in ((0, right), (1, left)):
            n = side * 4 + j
            b_copies[j, side] = remote(data, near(j, side), b_send.at[n], b_recv.at[n], peer)
            b_copies[j, side].start()

    send_along(0)
    exchange(1, 1, here16)
    exchange(0, 1, mate)
    own = pltpu.make_async_copy(staged.at[0], here16, local_sem.at[1])
    own.start()
    sort_rows(area, table)
    sorted_rows = pltpu.make_async_copy(table, src, local_sem.at[0])
    sorted_rows.start()
    a_copies[1].wait_recv()
    send_along(1)
    a_copies[0].wait_recv()
    sorted_rows.wait()

    weights = column_weights()
    q64 = [pl.multiple_of(tile(j) * 64, 64) for j in range(4)]

    def build_near(w, _):
        build_own(w, src, weights, staged.at[0], q64[0], lhs)
        build_own(w, src, weights, mate, q64[1], lhs)
        return 0

    lax.fori_loop(0, 16, build_near, 0, unroll=2)
    for j in (2, 3):
        a_copies[j].wait_recv()
        send_along(j)
    own.wait()

    def send_results(o, g):
        for j in (2, 3, 1, 0):
            p = tile(j)
            block, land = res.at[g, o * 4 + p], lands[g].at[k * 4 + q]
            away = remote(block, land, c_send.at[g], c_recv.at[g], (o, z * 4 + p))
            if j:
                away.start()
                continue

            @pl.when(o == k)
            def _():
                pltpu.make_async_copy(block, land, c_recv.at[g]).start()

            @pl.when(o != k)
            def _():
                away.start()

    def z0_tile(j):
        return z0.at[:, rows16(tile(j) * 16), :]

    def distant(n, u):
        x = (1 - (n // 2) * (1 - n // 3)) if u == 0 else (n % 2) * (1 - n // 3)
        y = 2 - (n + 1) // 2 if u == 0 else 2 + (n + 1) // 2
        return ((k // 4 + x) % 2) * 4 + (k + y) % 4

    def group(g):
        def windows(regions):
            pairs = [(o, o * 2 + h) for o in regions for h in range(2)]
            if g == 0:
                for _, w in pairs:
                    for j in (2, 3):
                        build_own(w, src, weights, z0_tile(j), q64[j], lhs)
            sums = [window_sums(w, src, weights, zs[g], lhs) for _, w in pairs]
            if g == 0:
                for (_, w), (_, intensity) in zip(pairs, sums):
                    own_intensities(w, intensity, own_power)
            for n, ((o, w), (full, intensity)) in enumerate(zip(pairs, sums)):
                h = n % 2
                block = coherence(full, intensity, own_power[w])
                res[g, pl.ds(o * 4, 4), h * 2 : h * 2 + 2] = block
                if h:
                    send_results(o, g)

        def step(n, _):
            windows([distant(n, 0), distant(n, 1)])
            return 0

        lax.fori_loop(0, 4, step, 0)

    group(0)
    for j in (0, 1):
        for side in range(2):
            b_copies[j, side].wait_recv()
    group(1)

    relays = []

    def relay(j):
        side, peer = ((0, right), (0, right), (1, left), (1, left))[j]
        n = 8 + j
        relays.append(remote(
            near(j, side), zs[3].at[:, rows16(tile(j) * 16), :], b_send.at[n], b_recv.at[n], peer
        ))
        relays[-1].start()

    for j in (2, 3):
        b_copies[j, 0].wait_recv()
        b_copies[j, 1].wait_recv()
        relay(j - 2)
        relay(j)
    group(2)
    for copy in relays:
        copy.wait_recv()
    group(3)

    for g in (1, 2):
        pltpu.make_async_copy(res.at[g], lands[g], c_recv.at[g]).wait()

    def turn(n, _):
        same = blocks_of(landed[0, pl.ds(n * 8, 8)])
        cross = blocks_of(landed[1, pl.ds(n * 8, 8)])
        near = jnp.concatenate([same[:, 0:2], cross[:, 2:4]], axis=1)
        far = jnp.concatenate([cross[:, 0:2], same[:, 2:4]], axis=1)
        side_by_side(near, far, mixed)
        for i in range(8):
            y = mixed[pl.ds(i, 128, stride=8), :].T
            for x in range(2):
                for side in range(2):
                    for part in range(2):
                        lane = x * 64 + side * 32 + part * 8
                        pair = jnp.concatenate([y[lane : lane + 8], y[lane + 16 : lane + 24]], axis=0)
                        built[n, part, i, side, x * 16 : x * 16 + 16, :] = pair.astype(BF16)
        columns = pl.ds(pl.multiple_of(n * 128, 128), 128)
        pltpu.make_async_copy(
            built.at[n], turned.at[:, :, :, :, columns], turn_sem.at[n]
        ).start()
        return 0

    lax.fori_loop(0, 4, turn, 0)

    for copy in list(a_copies.values()) + list(b_copies.values()) + relays:
        copy.wait_send()
    for n in range(4):
        columns = pl.ds(n * 128, 128)
        pltpu.make_async_copy(
            built.at[n], turned.at[:, :, :, :, columns], turn_sem.at[n]
        ).wait()
    for g in range(4):
        some = pl.ds(0, 31)
        pltpu.make_async_copy(res.at[g, some], lands[g].at[some], c_send.at[g]).wait()
    for g in (0, 3):
        pltpu.make_async_copy(res.at[g], lands[g], c_recv.at[g]).wait()


def finish_kernel(recv, turned, out, wide, built, mixed, write_sem, wide_sem):
    z = lax.axis_index("acq") // 4

    def rows_of(offset):
        return pl.ds(pl.multiple_of(((z + offset) % 4) * 32, 32), 32)

    copies = []

    def write(from_ref, to_ref, sem):
        copies.append(pltpu.make_async_copy(from_ref, to_ref, sem))
        copies[-1].start()

    for part in range(2):
        wide[part] = turned[part].astype(F32)
        for d in range(2):
            land = out.at[part, :, rows_of(3 + 2 * d)]
            write(wide.at[part, :, d], land, wide_sem.at[part, d])
    for n in range(4):
        some = slice(n * 8, n * 8 + 8)
        side_by_side(blocks_of(recv[0, some]), blocks_of(recv[1, some]), mixed)
        for i in range(8):
            y = mixed[pl.ds(i, 128, stride=8), :].T
            for t in range(8):
                for part in range(2):
                    lane, at = t * 16 + part * 8, (t % 4) * 8
                    built[n, t // 4, part, i, at : at + 8, :] = y[lane : lane + 8]
        columns = pl.ds(n * 128, 128)
        for d in range(2):
            write(built.at[n, d], out.at[:, :, rows_of(2 * d), columns], write_sem.at[n, d])
    for copy in copies:
        copy.wait()


def local(scene_lines, assigned_area):
    smem = pl.BlockSpec(memory_space=pltpu.SMEM)
    vmem = pl.BlockSpec(memory_space=pltpu.VMEM)
    hbm = pl.BlockSpec(memory_space=pltpu.HBM)
    blocks = (4, 32, 4, 16, 128)
    got = pl.pallas_call(
        pairs_kernel,
        out_shape=[
            jax.ShapeDtypeStruct((2, 32, 4, 16, 128), BF16),
            jax.ShapeDtypeStruct((2, 8, 2, 32, 512), BF16),
        ],
        in_specs=[smem, hbm],
        out_specs=[hbm, hbm],
        scratch_shapes=[
            pltpu.VMEM((4, 2, 8, 48, 128), BF16),
            pltpu.VMEM((4, 768, 128), F32),
            pltpu.VMEM((4, 48, 16, 128), BF16),
            pltpu.VMEM((48, 16, 128), BF16),
            pltpu.VMEM((2, 8, 128), jnp.int32),
            pltpu.SMEM((2, 8, 128), jnp.int32),
            pltpu.VMEM((48, 64, 128), BF16),
            pltpu.VMEM((48, 64, 128), BF16),
            pltpu.VMEM((48, 64, 128), BF16),
            pltpu.VMEM((48, 64, 128), BF16),
            pltpu.VMEM((16, 256, 512), BF16),
            pltpu.VMEM((16, 16, 8, 128), F32),
            pltpu.VMEM(blocks, BF16),
            pltpu.VMEM((2, 32, 4, 16, 128), BF16),
            pltpu.VMEM((1024, 128), F32),
            pltpu.VMEM((4, 2, 8, 2, 32, 128), BF16),
            pltpu.SemaphoreType.DMA((4,)),
            pltpu.SemaphoreType.DMA((2,)),
            pltpu.SemaphoreType.DMA((4,)),
            pltpu.SemaphoreType.DMA((4,)),
            pltpu.SemaphoreType.DMA((4,)),
            pltpu.SemaphoreType.DMA((12,)),
            pltpu.SemaphoreType.DMA((12,)),
            pltpu.SemaphoreType.DMA((4,)),
            pltpu.SemaphoreType.DMA((4,)),
        ],
        compiler_params=pltpu.CompilerParams(
            vmem_limit_bytes=40 << 20, collective_id=0, has_side_effects=True
        ),
    )(
        pltpu.with_memory_space_constraint(assigned_area.reshape(1, 48), pltpu.HBM),
        pltpu.with_memory_space_constraint(scene_lines, pltpu.HBM),
    )
    return pl.pallas_call(
        finish_kernel,
        out_shape=jax.ShapeDtypeStruct((2, 8, 128, 512), F32),
        in_specs=[vmem, vmem],
        out_specs=hbm,
        scratch_shapes=[
            pltpu.VMEM((2, 8, 2, 32, 512), F32),
            pltpu.VMEM((4, 2, 2, 8, 32, 128), F32),
            pltpu.VMEM((1024, 128), F32),
            pltpu.SemaphoreType.DMA((4, 2)),
            pltpu.SemaphoreType.DMA((2, 2)),
        ],
        compiler_params=pltpu.CompilerParams(vmem_limit_bytes=32 << 20),
    )(*got)


def solution(mesh):
    placed = (P(None, "acq", "region", None), P("region", None))
    return jax.shard_map(
        local, mesh=mesh, in_specs=placed, out_specs=P(None, "acq", None, "region"), check_vma=False
    )
```

```python
import jax
import jax.numpy as jnp
import numpy as np
from jax import lax
from jax.experimental import pallas as pl
from jax.experimental.pallas import tpu as pltpu
from jax.sharding import PartitionSpec as P

F32 = jnp.float32
BF16 = jnp.bfloat16
NT = (((1,), (1,)), ((), ()))
MESH = pl.DeviceIdType.MESH


def taper(length, centre, width):
    index = np.arange(length, dtype=np.float32)
    values = np.exp(np.float32(-0.5) * ((index - np.float32(centre)) / np.float32(width)) ** 2)
    return values / np.sum(values)


ROWS = [float(v) for v in taper(4, 1.5, 1.5)]
COLS = [float(v) for v in taper(16, 7.5, 5.0).astype(jnp.bfloat16).astype(np.float32)]


def lanes(shape):
    return lax.broadcasted_iota(jnp.int32, shape, len(shape) - 1)


def column_weights():
    col = lanes((8, 128))
    values = jnp.zeros((8, 128), F32)
    for k in range(16):
        values = jnp.where(col % 16 == k, COLS[k], values)
    return values


def swap_parts(x):
    up = pltpu.roll(x, 120, axis=x.ndim - 1)
    down = pltpu.roll(x, 8, axis=x.ndim - 1)
    return jnp.where((lanes(x.shape) // 8) % 2 == 0, up, down)


def sort_rows(area, table):
    slot = lanes((8, 128))
    owner, place = slot // 8, slot % 8
    source = jnp.zeros((8, 128), jnp.int32)
    held = jnp.zeros((8, 128), jnp.int32)
    count = jnp.zeros((8, 128), jnp.int32)
    for b in range(48):
        hit = owner == area[0, b]
        take = jnp.logical_and(hit, count == place)
        source = jnp.where(take, b, source)
        held = jnp.where(take, 1, held)
        count = count + hit.astype(jnp.int32)
    table[0] = source
    table[1] = held


def stage_columns(lines, wide, staged):
    for n in range(16):
        wide[n * 48 : (n + 1) * 48, :] = lines[n // 8, n % 8].astype(F32)

    def row(b, _):
        staged[b] = wide[pl.ds(b, 16, stride=48), :].astype(BF16)
        return 0

    lax.fori_loop(0, 48, row, 0, unroll=8)


def build_own(w, src, weights, rows, at, lhs):
    look = (lanes((8, 128)) // 16) % 4
    for r in range(4):
        s = w * 4 + r
        table = weights * (ROWS[r] * src[1, 0, s].astype(F32))
        own = rows[src[0, 0, s]].astype(F32).reshape(2, 8, 128)
        spread = jnp.stack([own * jnp.where(look == l, table, 0.0)[None] for l in range(4)], axis=0)
        lhs[w, pl.ds(at, 64), r * 128 : (r + 1) * 128] = spread.reshape(64, 128).astype(BF16)


def window_sums(w, src, weights, z, lhs):
    zero = jnp.zeros((64, 128), BF16)
    low = lanes((64, 128)) < 64
    look = (lanes((8, 128)) // 16) % 4 == lax.broadcasted_iota(jnp.int32, (8, 128), 0)
    data, power, looks = [], [], []
    for r in range(4):
        s = w * 4 + r
        row = z[src[0, 0, s]]
        square = row * row
        data.append(jnp.concatenate([jnp.where(low, row, zero), jnp.where(low, zero, row)], axis=0))
        power.append(
            jnp.concatenate([jnp.where(low, square, zero), jnp.where(low, zero, square)], axis=0)
        )
        table = weights * (ROWS[r] * src[1, 0, s].astype(F32))
        looks.append(jnp.where(look, table, 0.0).astype(BF16))
    data = jnp.concatenate(data, axis=1)
    power = jnp.concatenate(power, axis=1)
    looks = jnp.concatenate(looks, axis=1)
    full = lax.dot_general(lhs[w], data, NT, preferred_element_type=F32)
    halves = lax.dot_general(looks, power, NT, preferred_element_type=F32)
    return full, halves + swap_parts(halves)


def own_intensities(w, intensity, own_power):
    lane = lanes((8, 128))
    same = lane % 16 == lax.broadcasted_iota(jnp.int32, (8, 128), 0)
    picked = []
    for q in range(4):
        mine = jnp.logical_and(same, (lane // 16) % 4 == q)
        for l in range(4):
            row = jnp.broadcast_to(intensity[l : l + 1], (8, 128))
            picked.append(jnp.where(mine, row, 0.0))
    picked = jnp.concatenate(picked, axis=0)
    coarse = picked.astype(BF16)
    fine = (picked - coarse.astype(F32)).astype(BF16)
    terms = jnp.concatenate([coarse, fine], axis=1)
    lane = lanes((128, 256)) % 128
    half = lax.broadcasted_iota(jnp.int32, (128, 256), 0)
    spread = jnp.where((lane < 64) == (half < 64), 1.0, 0.0).astype(BF16)
    both = lax.dot_general(terms, spread, NT, preferred_element_type=F32)
    own_power[w] = both.reshape(16, 8, 128)


def coherence(full, intensity, own):
    full = full.reshape(16, 2, 8, 128)
    sign = jnp.where((lanes((8, 128)) // 8) % 2 == 0, 1.0, -1.0).astype(F32)
    swapped = swap_parts(full[:, 1].reshape(128, 128)).reshape(16, 8, 128)
    total = swapped + sign[None] * full[:, 0]
    other = jnp.stack([jnp.broadcast_to(intensity[l : l + 1], (8, 128)) for l in range(4)], axis=0)
    product = own.reshape(4, 4, 8, 128) * other[None]
    scale = lax.rsqrt(product + 1e-6)
    return (total.reshape(4, 4, 8, 128) * scale).reshape(4, 2, 16, 128).astype(BF16)


def side_by_side(x, y, mixed):
    low = lanes((8, 128)) < 64

    def half_turn(v):
        return pltpu.roll(v.reshape(512, 128), 64, axis=1).reshape(v.shape)

    first = jnp.where(low, x, half_turn(y))
    second = jnp.where(low, half_turn(x), y)
    both = jnp.stack([first, second], axis=3)
    both = both.transpose(0, 2, 1, 3, 4, 5, 6)
    mixed[...] = both.reshape(1024, 128)


def blocks_of(x):
    return x.astype(F32).reshape(2, 4, 2, 4, 8, 128)


def pairs_kernel(
    area, scene, recv, turned,
    lines, wide, staged, mate, table, src, z0, z1, z2, z3, lhs, own_power, res, landed, mixed, built,
    turn_sem, local_sem, read_sem, a_send, a_recv, b_send, b_recv, c_send, c_recv,
):
    zs = (z0, z1, z2, z3)
    lands = (recv.at[0], landed.at[0], landed.at[1], recv.at[1])
    k = lax.axis_index("region")
    acq = lax.axis_index("acq")
    z = acq // 4
    q = acq % 4
    xl, core = q // 2, q % 2
    right = (k, ((z + 1) % 4) * 4 + q)
    left = (k, ((z + 3) % 4) * 4 + q)

    def tile(j):
        return ((xl + j // 2) % 2) * 2 + (core + j % 2) % 2

    def rows16(start):
        return pl.ds(pl.multiple_of(start, 16), 16)

    reads = {}
    for j in (2, 3, 0, 1):
        columns = pl.ds(pl.multiple_of(tile(j) * 128, 128), 128)
        reads[j] = pltpu.make_async_copy(scene.at[:, :, :, columns], lines.at[j], read_sem.at[j])
        reads[j].start()
    barrier = pltpu.get_barrier_semaphore()
    for peer in (left, right):
        pl.semaphore_signal(barrier, inc=1, device_id=peer, device_id_type=MESH)

    for n in range(1, 32):
        o = ((k // 4 + n // 16) % 2) * 4 + (k + n // 4) % 4
        peer = (o, z * 4 + tile(n % 4))
        pl.semaphore_signal(barrier, inc=1, device_id=peer, device_id_type=MESH)

    for j in (2, 3):
        reads[j].wait()
        stage_columns(lines.at[j], wide.at[j], staged.at[j])
    pl.semaphore_wait(barrier, 33)

    def remote(from_ref, to_ref, send, recv, peer):
        return pltpu.make_async_remote_copy(
            src_ref=from_ref, dst_ref=to_ref, send_sem=send, recv_sem=recv,
            device_id=peer, device_id_type=MESH,
        )

    a_copies = {}

    def exchange(n, j, land):
        peer = (k, z * 4 + tile(j))
        a_copies[n] = remote(staged.at[j], land, a_send.at[n], a_recv.at[n], peer)
        a_copies[n].start()

    here16 = z0.at[:, rows16(q * 16), :]
    exchange(2, 2, here16)
    exchange(3, 3, here16)
    for j in (0, 1):
        reads[j].wait()
        stage_columns(lines.at[j], wide.at[j], staged.at[j])

    def near(j, side):
        return zs[1 + j // 2].at[:, rows16(side * 32 + ((core + j) % 2) * 16), :]

    b_copies = {}

    def send_along(j):
        data = staged.at[0] if j == 0 else zs[0].at[:, rows16(tile(j) * 16), :]
        for side, peer in ((0, right), (1, left)):
            n = side * 4 + j
            b_copies[j, side] = remote(data, near(j, side), b_send.at[n], b_recv.at[n], peer)
            b_copies[j, side].start()

    send_along(0)
    exchange(1, 1, here16)
    exchange(0, 1, mate)
    own = pltpu.make_async_copy(staged.at[0], here16, local_sem.at[1])
    own.start()
    sort_rows(area, table)
    sorted_rows = pltpu.make_async_copy(table, src, local_sem.at[0])
    sorted_rows.start()
    a_copies[1].wait_recv()
    send_along(1)
    a_copies[0].wait_recv()
    sorted_rows.wait()

    weights = column_weights()
    q64 = [pl.multiple_of(tile(j) * 64, 64) for j in range(4)]

    def build_near(w, _):
        build_own(w, src, weights, staged.at[0], q64[0], lhs)
        build_own(w, src, weights, mate, q64[1], lhs)
        return 0

    lax.fori_loop(0, 16, build_near, 0, unroll=2)
    relays = []

    def relay(j):
        side, peer = ((0, right), (1, left), (0, right), (1, left))[j]
        n = 8 + j
        relays.append(remote(
            near(j, side), zs[3].at[:, rows16(tile(j) * 16), :], b_send.at[n], b_recv.at[n], peer
        ))
        relays[-1].start()

    for j in (2, 3):
        a_copies[j].wait_recv()
        send_along(j)
    own.wait()

    def send_results(o, g):
        for j in (2, 3, 1, 0):
            p = tile(j)
            block, land = res.at[g, o * 4 + p], lands[g].at[k * 4 + q]
            away = remote(block, land, c_send.at[g], c_recv.at[g], (o, z * 4 + p))
            if j:
                away.start()
                continue

            @pl.when(o == k)
            def _():
                pltpu.make_async_copy(block, land, c_recv.at[g]).start()

            @pl.when(o != k)
            def _():
                away.start()

    def z0_tile(j):
        return z0.at[:, rows16(tile(j) * 16), :]

    def distant(n, u):
        x = (1 - (n // 2) * (1 - n // 3)) if u == 0 else (n % 2) * (1 - n // 3)
        y = 2 - (n + 1) // 2 if u == 0 else 2 + (n + 1) // 2
        return ((k // 4 + x) % 2) * 4 + (k + y) % 4

    def group(g):
        def windows(regions):
            pairs = [(o, o * 2 + h) for o in regions for h in range(2)]
            if g == 0:
                for _, w in pairs:
                    for j in (2, 3):
                        build_own(w, src, weights, z0_tile(j), q64[j], lhs)
            sums = [window_sums(w, src, weights, zs[g], lhs) for _, w in pairs]
            if g == 0:
                for (_, w), (_, intensity) in zip(pairs, sums):
                    own_intensities(w, intensity, own_power)
            for n, ((o, w), (full, intensity)) in enumerate(zip(pairs, sums)):
                h = n % 2
                block = coherence(full, intensity, own_power[w])
                res[g, pl.ds(o * 4, 4), h * 2 : h * 2 + 2] = block
                if h:
                    send_results(o, g)

        def step(n, _):
            windows([distant(n, 0), distant(n, 1)])
            return 0

        lax.fori_loop(0, 4, step, 0)

    group(0)
    for j in (0, 1):
        for side in range(2):
            b_copies[j, side].wait_recv()
    relay(0)
    relay(1)
    group(1)

    for j in (2, 3):
        b_copies[j, 0].wait_recv()
        b_copies[j, 1].wait_recv()
        relay(j)
    group(2)
    for copy in relays:
        copy.wait_recv()
    group(3)

    for g in (1, 2):
        pltpu.make_async_copy(res.at[g], lands[g], c_recv.at[g]).wait()

    def turn(n, _):
        same = blocks_of(landed[0, pl.ds(n * 8, 8)])
        cross = blocks_of(landed[1, pl.ds(n * 8, 8)])
        near = jnp.concatenate([same[:, 0:2], cross[:, 2:4]], axis=1)
        far = jnp.concatenate([cross[:, 0:2], same[:, 2:4]], axis=1)
        side_by_side(near, far, mixed)
        for i in range(8):
            y = mixed[pl.ds(i, 128, stride=8), :].T
            for x in range(2):
                for side in range(2):
                    for part in range(2):
                        lane = x * 64 + side * 32 + part * 8
                        pair = jnp.concatenate([y[lane : lane + 8], y[lane + 16 : lane + 24]], axis=0)
                        built[n, part, i, side, x * 16 : x * 16 + 16, :] = pair.astype(BF16)
        columns = pl.ds(pl.multiple_of(n * 128, 128), 128)
        pltpu.make_async_copy(
            built.at[n], turned.at[:, :, :, :, columns], turn_sem.at[n]
        ).start()
        return 0

    lax.fori_loop(0, 4, turn, 0)

    for copy in list(a_copies.values()) + list(b_copies.values()) + relays:
        copy.wait_send()
    for n in range(4):
        columns = pl.ds(n * 128, 128)
        pltpu.make_async_copy(
            built.at[n], turned.at[:, :, :, :, columns], turn_sem.at[n]
        ).wait()
    for g in range(4):
        some = pl.ds(0, 31)
        pltpu.make_async_copy(res.at[g, some], lands[g].at[some], c_send.at[g]).wait()
    for g in (0, 3):
        pltpu.make_async_copy(res.at[g], lands[g], c_recv.at[g]).wait()


def finish_kernel(recv, turned, out, wide, built, mixed, write_sem, wide_sem):
    z = lax.axis_index("acq") // 4

    def rows_of(offset):
        return pl.ds(pl.multiple_of(((z + offset) % 4) * 32, 32), 32)

    copies = []

    def write(from_ref, to_ref, sem):
        copies.append(pltpu.make_async_copy(from_ref, to_ref, sem))
        copies[-1].start()

    for part in range(2):
        wide[part] = turned[part].astype(F32)
        for d in range(2):
            land = out.at[part, :, rows_of(3 + 2 * d)]
            write(wide.at[part, :, d], land, wide_sem.at[part, d])
    for n in range(4):
        some = slice(n * 8, n * 8 + 8)
        side_by_side(blocks_of(recv[0, some]), blocks_of(recv[1, some]), mixed)
        for i in range(8):
            y = mixed[pl.ds(i, 128, stride=8), :].T
            for t in range(8):
                for part in range(2):
                    lane, at = t * 16 + part * 8, (t % 4) * 8
                    built[n, t // 4, part, i, at : at + 8, :] = y[lane : lane + 8]
        columns = pl.ds(n * 128, 128)
        for d in range(2):
            write(built.at[n, d], out.at[:, :, rows_of(2 * d), columns], write_sem.at[n, d])
    for copy in copies:
        copy.wait()


def local(scene_lines, assigned_area):
    smem = pl.BlockSpec(memory_space=pltpu.SMEM)
    vmem = pl.BlockSpec(memory_space=pltpu.VMEM)
    hbm = pl.BlockSpec(memory_space=pltpu.HBM)
    blocks = (4, 32, 4, 16, 128)
    got = pl.pallas_call(
        pairs_kernel,
        out_shape=[
            jax.ShapeDtypeStruct((2, 32, 4, 16, 128), BF16),
            jax.ShapeDtypeStruct((2, 8, 2, 32, 512), BF16),
        ],
        in_specs=[smem, hbm],
        out_specs=[hbm, hbm],
        scratch_shapes=[
            pltpu.VMEM((4, 2, 8, 48, 128), BF16),
            pltpu.VMEM((4, 768, 128), F32),
            pltpu.VMEM((4, 48, 16, 128), BF16),
            pltpu.VMEM((48, 16, 128), BF16),
            pltpu.VMEM((2, 8, 128), jnp.int32),
            pltpu.SMEM((2, 8, 128), jnp.int32),
            pltpu.VMEM((48, 64, 128), BF16),
            pltpu.VMEM((48, 64, 128), BF16),
            pltpu.VMEM((48, 64, 128), BF16),
            pltpu.VMEM((48, 64, 128), BF16),
            pltpu.VMEM((16, 256, 512), BF16),
            pltpu.VMEM((16, 16, 8, 128), F32),
            pltpu.VMEM(blocks, BF16),
            pltpu.VMEM((2, 32, 4, 16, 128), BF16),
            pltpu.VMEM((1024, 128), F32),
            pltpu.VMEM((4, 2, 8, 2, 32, 128), BF16),
            pltpu.SemaphoreType.DMA((4,)),
            pltpu.SemaphoreType.DMA((2,)),
            pltpu.SemaphoreType.DMA((4,)),
            pltpu.SemaphoreType.DMA((4,)),
            pltpu.SemaphoreType.DMA((4,)),
            pltpu.SemaphoreType.DMA((12,)),
            pltpu.SemaphoreType.DMA((12,)),
            pltpu.SemaphoreType.DMA((4,)),
            pltpu.SemaphoreType.DMA((4,)),
        ],
        compiler_params=pltpu.CompilerParams(
            vmem_limit_bytes=40 << 20, collective_id=0, has_side_effects=True
        ),
    )(
        pltpu.with_memory_space_constraint(assigned_area.reshape(1, 48), pltpu.HBM),
        pltpu.with_memory_space_constraint(scene_lines, pltpu.HBM),
    )
    return pl.pallas_call(
        finish_kernel,
        out_shape=jax.ShapeDtypeStruct((2, 8, 128, 512), F32),
        in_specs=[vmem, vmem],
        out_specs=hbm,
        scratch_shapes=[
            pltpu.VMEM((2, 8, 2, 32, 512), F32),
            pltpu.VMEM((4, 2, 2, 8, 32, 128), F32),
            pltpu.VMEM((1024, 128), F32),
            pltpu.SemaphoreType.DMA((4, 2)),
            pltpu.SemaphoreType.DMA((2, 2)),
        ],
        compiler_params=pltpu.CompilerParams(vmem_limit_bytes=32 << 20),
    )(*got)


def solution(mesh):
    placed = (P(None, "acq", "region", None), P("region", None))
    return jax.shard_map(
        local, mesh=mesh, in_specs=placed, out_specs=P(None, "acq", None, "region"), check_vma=False
    )
```

```python
import jax
import jax.numpy as jnp
import numpy as np
from jax import lax
from jax.experimental import pallas as pl
from jax.experimental.pallas import tpu as pltpu
from jax.sharding import PartitionSpec as P

F32 = jnp.float32
BF16 = jnp.bfloat16
NT = (((1,), (1,)), ((), ()))
MESH = pl.DeviceIdType.MESH


def taper(length, centre, width):
    index = np.arange(length, dtype=np.float32)
    values = np.exp(np.float32(-0.5) * ((index - np.float32(centre)) / np.float32(width)) ** 2)
    return values / np.sum(values)


ROWS = [float(v) for v in taper(4, 1.5, 1.5)]
COLS = [float(v) for v in taper(16, 7.5, 5.0).astype(jnp.bfloat16).astype(np.float32)]


def lanes(shape):
    return lax.broadcasted_iota(jnp.int32, shape, len(shape) - 1)


def column_weights():
    col = lanes((8, 128))
    values = jnp.zeros((8, 128), F32)
    for k in range(16):
        values = jnp.where(col % 16 == k, COLS[k], values)
    return values


def swap_parts(x):
    up = pltpu.roll(x, 120, axis=x.ndim - 1)
    down = pltpu.roll(x, 8, axis=x.ndim - 1)
    return jnp.where((lanes(x.shape) // 8) % 2 == 0, up, down)


def sort_rows(area, table):
    slot = lanes((8, 128))
    owner, place = slot // 8, slot % 8
    source = jnp.zeros((8, 128), jnp.int32)
    held = jnp.zeros((8, 128), jnp.int32)
    count = jnp.zeros((8, 128), jnp.int32)
    for b in range(48):
        hit = owner == area[0, b]
        take = jnp.logical_and(hit, count == place)
        source = jnp.where(take, b, source)
        held = jnp.where(take, 1, held)
        count = count + hit.astype(jnp.int32)
    table[0] = source
    table[1] = held


def stage_columns(lines, wide, staged):
    for n in range(16):
        wide[n * 48 : (n + 1) * 48, :] = lines[n // 8, n % 8].astype(F32)

    def row(b, _):
        staged[b] = wide[pl.ds(b, 16, stride=48), :].astype(BF16)
        return 0

    lax.fori_loop(0, 48, row, 0, unroll=8)


def build_own(w, src, weights, rows, at, lhs):
    look = (lanes((8, 128)) // 16) % 4
    for r in range(4):
        s = w * 4 + r
        table = weights * (ROWS[r] * src[1, 0, s].astype(F32))
        own = rows[src[0, 0, s]].astype(F32).reshape(2, 8, 128)
        spread = jnp.stack([own * jnp.where(look == l, table, 0.0)[None] for l in range(4)], axis=0)
        lhs[w, pl.ds(at, 64), r * 128 : (r + 1) * 128] = spread.reshape(64, 128).astype(BF16)


def window_sums(w, src, weights, z, lhs):
    zero = jnp.zeros((64, 128), BF16)
    low = lanes((64, 128)) < 64
    look = (lanes((8, 128)) // 16) % 4 == lax.broadcasted_iota(jnp.int32, (8, 128), 0)
    data, power, looks = [], [], []
    for r in range(4):
        s = w * 4 + r
        row = z[src[0, 0, s]]
        square = row * row
        data.append(jnp.concatenate([jnp.where(low, row, zero), jnp.where(low, zero, row)], axis=0))
        power.append(
            jnp.concatenate([jnp.where(low, square, zero), jnp.where(low, zero, square)], axis=0)
        )
        table = weights * (ROWS[r] * src[1, 0, s].astype(F32))
        looks.append(jnp.where(look, table, 0.0).astype(BF16))
    data = jnp.concatenate(data, axis=1)
    power = jnp.concatenate(power, axis=1)
    looks = jnp.concatenate(looks, axis=1)
    full = lax.dot_general(lhs[w], data, NT, preferred_element_type=F32)
    halves = lax.dot_general(looks, power, NT, preferred_element_type=F32)
    return full, halves + swap_parts(halves)


def own_intensities(w, intensity, own_power):
    lane = lanes((8, 128))
    same = lane % 16 == lax.broadcasted_iota(jnp.int32, (8, 128), 0)
    picked = []
    for q in range(4):
        mine = jnp.logical_and(same, (lane // 16) % 4 == q)
        for l in range(4):
            row = jnp.broadcast_to(intensity[l : l + 1], (8, 128))
            picked.append(jnp.where(mine, row, 0.0))
    picked = jnp.concatenate(picked, axis=0)
    coarse = picked.astype(BF16)
    fine = (picked - coarse.astype(F32)).astype(BF16)
    terms = jnp.concatenate([coarse, fine], axis=1)
    lane = lanes((128, 256)) % 128
    half = lax.broadcasted_iota(jnp.int32, (128, 256), 0)
    spread = jnp.where((lane < 64) == (half < 64), 1.0, 0.0).astype(BF16)
    both = lax.dot_general(terms, spread, NT, preferred_element_type=F32)
    own_power[w] = both.reshape(16, 8, 128)


def coherence(full, intensity, own):
    full = full.reshape(16, 2, 8, 128)
    sign = jnp.where((lanes((8, 128)) // 8) % 2 == 0, 1.0, -1.0).astype(F32)
    swapped = swap_parts(full[:, 1].reshape(128, 128)).reshape(16, 8, 128)
    total = swapped + sign[None] * full[:, 0]
    other = jnp.stack([jnp.broadcast_to(intensity[l : l + 1], (8, 128)) for l in range(4)], axis=0)
    product = own.reshape(4, 4, 8, 128) * other[None]
    scale = lax.rsqrt(product + 1e-6)
    return (total.reshape(4, 4, 8, 128) * scale).reshape(4, 2, 16, 128).astype(BF16)


def side_by_side(x, y, mixed):
    low = lanes((8, 128)) < 64

    def half_turn(v):
        return pltpu.roll(v.reshape(512, 128), 64, axis=1).reshape(v.shape)

    first = jnp.where(low, x, half_turn(y))
    second = jnp.where(low, half_turn(x), y)
    both = jnp.stack([first, second], axis=3)
    both = both.transpose(0, 2, 1, 3, 4, 5, 6)
    mixed[...] = both.reshape(1024, 128)


def blocks_of(x):
    return x.astype(F32).reshape(2, 4, 2, 4, 8, 128)


def pairs_kernel(
    area, scene, recv, turned,
    lines, wide, staged, mate, table, src, z0, z1, z2, z3, lhs, own_power, res, landed, mixed, built,
    turn_sem, local_sem, read_sem, a_send, a_recv, b_send, b_recv, c_send, c_recv,
):
    zs = (z0, z1, z2, z3)
    lands = (recv.at[0], landed.at[0], landed.at[1], recv.at[1])
    k = lax.axis_index("region")
    acq = lax.axis_index("acq")
    z = acq // 4
    q = acq % 4
    xl, core = q // 2, q % 2
    right = (k, ((z + 1) % 4) * 4 + q)
    left = (k, ((z + 3) % 4) * 4 + q)

    def tile(j):
        return ((xl + j // 2) % 2) * 2 + (core + j % 2) % 2

    def rows16(start):
        return pl.ds(pl.multiple_of(start, 16), 16)

    reads = {}
    for j in (2, 3, 0, 1):
        columns = pl.ds(pl.multiple_of(tile(j) * 128, 128), 128)
        reads[j] = pltpu.make_async_copy(scene.at[:, :, :, columns], lines.at[j], read_sem.at[j])
        reads[j].start()
    barrier = pltpu.get_barrier_semaphore()
    for peer in (left, right):
        pl.semaphore_signal(barrier, inc=1, device_id=peer, device_id_type=MESH)

    for n in range(1, 32):
        o = ((k // 4 + n // 16) % 2) * 4 + (k + n // 4) % 4
        peer = (o, z * 4 + tile(n % 4))
        pl.semaphore_signal(barrier, inc=1, device_id=peer, device_id_type=MESH)

    for j in (2, 3):
        reads[j].wait()
        stage_columns(lines.at[j], wide.at[j], staged.at[j])
    pl.semaphore_wait(barrier, 33)

    def remote(from_ref, to_ref, send, recv, peer):
        return pltpu.make_async_remote_copy(
            src_ref=from_ref, dst_ref=to_ref, send_sem=send, recv_sem=recv,
            device_id=peer, device_id_type=MESH,
        )

    a_copies = {}

    def exchange(n, j, land):
        peer = (k, z * 4 + tile(j))
        a_copies[n] = remote(staged.at[j], land, a_send.at[n], a_recv.at[n], peer)
        a_copies[n].start()

    here16 = z0.at[:, rows16(q * 16), :]
    exchange(2, 2, here16)
    exchange(3, 3, here16)
    for j in (0, 1):
        reads[j].wait()
        stage_columns(lines.at[j], wide.at[j], staged.at[j])

    def near(j, side):
        return zs[1 + j // 2].at[:, rows16(side * 32 + ((core + j) % 2) * 16), :]

    b_copies = {}

    def send_along(j):
        data = staged.at[0] if j == 0 else zs[0].at[:, rows16(tile(j) * 16), :]
        for side, peer in ((0, right), (1, left)):
            n = side * 4 + j
            b_copies[j, side] = remote(data, near(j, side), b_send.at[n], b_recv.at[n], peer)
            b_copies[j, side].start()

    send_along(0)
    exchange(1, 1, here16)
    exchange(0, 1, mate)
    own = pltpu.make_async_copy(staged.at[0], here16, local_sem.at[1])
    own.start()
    sort_rows(area, table)
    sorted_rows = pltpu.make_async_copy(table, src, local_sem.at[0])
    sorted_rows.start()
    a_copies[1].wait_recv()
    send_along(1)
    a_copies[0].wait_recv()
    sorted_rows.wait()

    weights = column_weights()
    q64 = [pl.multiple_of(tile(j) * 64, 64) for j in range(4)]

    def build_near(w, _):
        build_own(w, src, weights, staged.at[0], q64[0], lhs)
        build_own(w, src, weights, mate, q64[1], lhs)
        return 0

    lax.fori_loop(0, 16, build_near, 0, unroll=2)
    relays = []

    def relay(j):
        side, peer = ((0, right), (1, left), (0, right), (1, left))[j]
        n = 8 + j
        relays.append(remote(
            near(j, side), zs[3].at[:, rows16(tile(j) * 16), :], b_send.at[n], b_recv.at[n], peer
        ))
        relays[-1].start()

    for j in (2, 3):
        a_copies[j].wait_recv()
        send_along(j)
    own.wait()

    def send_results(o, g):
        for j in (2, 3, 1, 0):
            p = tile(j)
            block, land = res.at[g, o * 4 + p], lands[g].at[k * 4 + q]
            away = remote(block, land, c_send.at[g], c_recv.at[g], (o, z * 4 + p))
            if j:
                away.start()
                continue

            @pl.when(o == k)
            def _():
                pltpu.make_async_copy(block, land, c_recv.at[g]).start()

            @pl.when(o != k)
            def _():
                away.start()

    def z0_tile(j):
        return z0.at[:, rows16(tile(j) * 16), :]

    def distant(n, u):
        x = (1 - (n // 2) * (1 - n // 3)) if u == 0 else (n % 2) * (1 - n // 3)
        y = 2 - (n + 1) // 2 if u == 0 else 2 + (n + 1) // 2
        return ((k // 4 + x) % 2) * 4 + (k + y) % 4

    def group(g):
        def windows(regions):
            pairs = [(o, o * 2 + h) for o in regions for h in range(2)]
            if g == 0:
                for _, w in pairs:
                    for j in (2, 3):
                        build_own(w, src, weights, z0_tile(j), q64[j], lhs)
            sums = [window_sums(w, src, weights, zs[g], lhs) for _, w in pairs]
            if g == 0:
                for (_, w), (_, intensity) in zip(pairs, sums):
                    own_intensities(w, intensity, own_power)
            for n, ((o, w), (full, intensity)) in enumerate(zip(pairs, sums)):
                h = n % 2
                block = coherence(full, intensity, own_power[w])
                res[g, pl.ds(o * 4, 4), h * 2 : h * 2 + 2] = block
                if h:
                    send_results(o, g)

        def step(n, _):
            windows([distant(n, 0), distant(n, 1)])
            return 0

        lax.fori_loop(0, 4, step, 0)

    group(0)
    for j in (0, 1):
        for side in range(2):
            b_copies[j, side].wait_recv()
    relay(0)
    relay(1)
    group(1)

    for j in (2, 3):
        b_copies[j, j - 2].wait_recv()
        relay(j)
    for j in (2, 3):
        b_copies[j, 3 - j].wait_recv()
    group(2)
    for copy in relays:
        copy.wait_recv()
    group(3)

    for g in (1, 2):
        pltpu.make_async_copy(res.at[g], lands[g], c_recv.at[g]).wait()

    def turn(n, _):
        same = blocks_of(landed[0, pl.ds(n * 8, 8)])
        cross = blocks_of(landed[1, pl.ds(n * 8, 8)])
        near = jnp.concatenate([same[:, 0:2], cross[:, 2:4]], axis=1)
        far = jnp.concatenate([cross[:, 0:2], same[:, 2:4]], axis=1)
        side_by_side(near, far, mixed)
        for i in range(8):
            y = mixed[pl.ds(i, 128, stride=8), :].T
            for x in range(2):
                for side in range(2):
                    for part in range(2):
                        lane = x * 64 + side * 32 + part * 8
                        pair = jnp.concatenate([y[lane : lane + 8], y[lane + 16 : lane + 24]], axis=0)
                        built[n, part, i, side, x * 16 : x * 16 + 16, :] = pair
        columns = pl.ds(pl.multiple_of(n * 128, 128), 128)
        pltpu.make_async_copy(
            built.at[n], turned.at[:, :, :, :, columns], turn_sem.at[n]
        ).start()
        return 0

    lax.fori_loop(0, 4, turn, 0)

    for copy in list(a_copies.values()) + list(b_copies.values()) + relays:
        copy.wait_send()
    for n in range(4):
        columns = pl.ds(n * 128, 128)
        pltpu.make_async_copy(
            built.at[n], turned.at[:, :, :, :, columns], turn_sem.at[n]
        ).wait()
    for g in range(4):
        some = pl.ds(0, 31)
        pltpu.make_async_copy(res.at[g, some], lands[g].at[some], c_send.at[g]).wait()
    for g in (0, 3):
        pltpu.make_async_copy(res.at[g], lands[g], c_recv.at[g]).wait()


def finish_kernel(recv, turned, out, built, mixed, write_sem, wide_sem):
    z = lax.axis_index("acq") // 4

    def rows_of(offset):
        return pl.ds(pl.multiple_of(((z + offset) % 4) * 32, 32), 32)

    copies = []

    def write(from_ref, to_ref, sem):
        copies.append(pltpu.make_async_copy(from_ref, to_ref, sem))
        copies[-1].start()

    for part in range(2):
        for d in range(2):
            land = out.at[part, :, rows_of(3 + 2 * d)]
            write(turned.at[part, :, d], land, wide_sem.at[part, d])
    for n in range(4):
        some = slice(n * 8, n * 8 + 8)
        side_by_side(blocks_of(recv[0, some]), blocks_of(recv[1, some]), mixed)
        for i in range(8):
            y = mixed[pl.ds(i, 128, stride=8), :].T
            for t in range(8):
                for part in range(2):
                    lane, at = t * 16 + part * 8, (t % 4) * 8
                    built[n, t // 4, part, i, at : at + 8, :] = y[lane : lane + 8]
        columns = pl.ds(n * 128, 128)
        for d in range(2):
            write(built.at[n, d], out.at[:, :, rows_of(2 * d), columns], write_sem.at[n, d])
    for copy in copies:
        copy.wait()


def local(scene_lines, assigned_area):
    smem = pl.BlockSpec(memory_space=pltpu.SMEM)
    vmem = pl.BlockSpec(memory_space=pltpu.VMEM)
    hbm = pl.BlockSpec(memory_space=pltpu.HBM)
    blocks = (4, 32, 4, 16, 128)
    got = pl.pallas_call(
        pairs_kernel,
        out_shape=[
            jax.ShapeDtypeStruct((2, 32, 4, 16, 128), BF16),
            jax.ShapeDtypeStruct((2, 8, 2, 32, 512), F32),
        ],
        in_specs=[smem, hbm],
        out_specs=[hbm, hbm],
        scratch_shapes=[
            pltpu.VMEM((4, 2, 8, 48, 128), BF16),
            pltpu.VMEM((4, 768, 128), F32),
            pltpu.VMEM((4, 48, 16, 128), BF16),
            pltpu.VMEM((48, 16, 128), BF16),
            pltpu.VMEM((2, 8, 128), jnp.int32),
            pltpu.SMEM((2, 8, 128), jnp.int32),
            pltpu.VMEM((48, 64, 128), BF16),
            pltpu.VMEM((48, 64, 128), BF16),
            pltpu.VMEM((48, 64, 128), BF16),
            pltpu.VMEM((48, 64, 128), BF16),
            pltpu.VMEM((16, 256, 512), BF16),
            pltpu.VMEM((16, 16, 8, 128), F32),
            pltpu.VMEM(blocks, BF16),
            pltpu.VMEM((2, 32, 4, 16, 128), BF16),
            pltpu.VMEM((1024, 128), F32),
            pltpu.VMEM((4, 2, 8, 2, 32, 128), F32),
            pltpu.SemaphoreType.DMA((4,)),
            pltpu.SemaphoreType.DMA((2,)),
            pltpu.SemaphoreType.DMA((4,)),
            pltpu.SemaphoreType.DMA((4,)),
            pltpu.SemaphoreType.DMA((4,)),
            pltpu.SemaphoreType.DMA((12,)),
            pltpu.SemaphoreType.DMA((12,)),
            pltpu.SemaphoreType.DMA((4,)),
            pltpu.SemaphoreType.DMA((4,)),
        ],
        compiler_params=pltpu.CompilerParams(
            vmem_limit_bytes=40 << 20, collective_id=0, has_side_effects=True
        ),
    )(
        pltpu.with_memory_space_constraint(assigned_area.reshape(1, 48), pltpu.HBM),
        pltpu.with_memory_space_constraint(scene_lines, pltpu.HBM),
    )
    return pl.pallas_call(
        finish_kernel,
        out_shape=jax.ShapeDtypeStruct((2, 8, 128, 512), F32),
        in_specs=[vmem, vmem],
        out_specs=hbm,
        scratch_shapes=[
            pltpu.VMEM((4, 2, 2, 8, 32, 128), F32),
            pltpu.VMEM((1024, 128), F32),
            pltpu.SemaphoreType.DMA((4, 2)),
            pltpu.SemaphoreType.DMA((2, 2)),
        ],
        compiler_params=pltpu.CompilerParams(vmem_limit_bytes=32 << 20),
    )(*got)


def solution(mesh):
    placed = (P(None, "acq", "region", None), P("region", None))
    return jax.shard_map(
        local, mesh=mesh, in_specs=placed, out_specs=P(None, "acq", None, "region"), check_vma=False
    )
```

```python
import jax
import jax.numpy as jnp
import numpy as np
from jax import lax
from jax.experimental import pallas as pl
from jax.experimental.pallas import tpu as pltpu
from jax.sharding import PartitionSpec as P

F32 = jnp.float32
BF16 = jnp.bfloat16
NT = (((1,), (1,)), ((), ()))
MESH = pl.DeviceIdType.MESH


def taper(length, centre, width):
    index = np.arange(length, dtype=np.float32)
    values = np.exp(np.float32(-0.5) * ((index - np.float32(centre)) / np.float32(width)) ** 2)
    return values / np.sum(values)


ROWS = [float(v) for v in taper(4, 1.5, 1.5)]
COLS = [float(v) for v in taper(16, 7.5, 5.0).astype(jnp.bfloat16).astype(np.float32)]


def lanes(shape):
    return lax.broadcasted_iota(jnp.int32, shape, len(shape) - 1)


def column_weights():
    col = lanes((8, 128))
    values = jnp.zeros((8, 128), F32)
    for k in range(16):
        values = jnp.where(col % 16 == k, COLS[k], values)
    return values


def swap_parts(x):
    up = pltpu.roll(x, 120, axis=x.ndim - 1)
    down = pltpu.roll(x, 8, axis=x.ndim - 1)
    return jnp.where((lanes(x.shape) // 8) % 2 == 0, up, down)


def sort_rows(area, table):
    slot = lanes((8, 128))
    owner, place = slot // 8, slot % 8
    source = jnp.zeros((8, 128), jnp.int32)
    held = jnp.zeros((8, 128), jnp.int32)
    count = jnp.zeros((8, 128), jnp.int32)
    for b in range(48):
        hit = owner == area[0, b]
        take = jnp.logical_and(hit, count == place)
        source = jnp.where(take, b, source)
        held = jnp.where(take, 1, held)
        count = count + hit.astype(jnp.int32)
    table[0] = source
    table[1] = held


def stage_columns(lines, wide, staged):
    for n in range(16):
        wide[n * 48 : (n + 1) * 48, :] = lines[n // 8, n % 8].astype(F32)

    def row(b, _):
        staged[b] = wide[pl.ds(b, 16, stride=48), :].astype(BF16)
        return 0

    lax.fori_loop(0, 48, row, 0, unroll=8)


def build_own(w, src, weights, rows, at, lhs):
    look = (lanes((8, 128)) // 16) % 4
    for r in range(4):
        s = w * 4 + r
        table = weights * (ROWS[r] * src[1, 0, s].astype(F32))
        own = rows[src[0, 0, s]].astype(F32).reshape(2, 8, 128)
        spread = jnp.stack([own * jnp.where(look == l, table, 0.0)[None] for l in range(4)], axis=0)
        lhs[w, pl.ds(at, 64), r * 128 : (r + 1) * 128] = spread.reshape(64, 128).astype(BF16)


def window_sums(w, src, weights, z, lhs):
    zero = jnp.zeros((64, 128), BF16)
    low = lanes((64, 128)) < 64
    look = (lanes((8, 128)) // 16) % 4 == lax.broadcasted_iota(jnp.int32, (8, 128), 0)
    data, power, looks = [], [], []
    for r in range(4):
        s = w * 4 + r
        row = z[src[0, 0, s]]
        square = row * row
        data.append(jnp.concatenate([jnp.where(low, row, zero), jnp.where(low, zero, row)], axis=0))
        power.append(
            jnp.concatenate([jnp.where(low, square, zero), jnp.where(low, zero, square)], axis=0)
        )
        table = weights * (ROWS[r] * src[1, 0, s].astype(F32))
        looks.append(jnp.where(look, table, 0.0).astype(BF16))
    data = jnp.concatenate(data, axis=1)
    power = jnp.concatenate(power, axis=1)
    looks = jnp.concatenate(looks, axis=1)
    full = lax.dot_general(lhs[w], data, NT, preferred_element_type=F32)
    halves = lax.dot_general(looks, power, NT, preferred_element_type=F32)
    return full, halves + swap_parts(halves)


def own_intensities(w, intensity, own_power):
    lane = lanes((8, 128))
    same = lane % 16 == lax.broadcasted_iota(jnp.int32, (8, 128), 0)
    picked = []
    for q in range(4):
        mine = jnp.logical_and(same, (lane // 16) % 4 == q)
        for l in range(4):
            row = jnp.broadcast_to(intensity[l : l + 1], (8, 128))
            picked.append(jnp.where(mine, row, 0.0))
    picked = jnp.concatenate(picked, axis=0)
    coarse = picked.astype(BF16)
    fine = (picked - coarse.astype(F32)).astype(BF16)
    terms = jnp.concatenate([coarse, fine], axis=1)
    lane = lanes((128, 256)) % 128
    half = lax.broadcasted_iota(jnp.int32, (128, 256), 0)
    spread = jnp.where((lane < 64) == (half < 64), 1.0, 0.0).astype(BF16)
    both = lax.dot_general(terms, spread, NT, preferred_element_type=F32)
    own_power[w] = both.reshape(16, 8, 128)


def coherence(full, intensity, own):
    full = full.reshape(16, 2, 8, 128)
    sign = jnp.where((lanes((8, 128)) // 8) % 2 == 0, 1.0, -1.0).astype(F32)
    swapped = swap_parts(full[:, 1].reshape(128, 128)).reshape(16, 8, 128)
    total = swapped + sign[None] * full[:, 0]
    other = jnp.stack([jnp.broadcast_to(intensity[l : l + 1], (8, 128)) for l in range(4)], axis=0)
    product = own.reshape(4, 4, 8, 128) * other[None]
    scale = lax.rsqrt(product + 1e-6)
    return (total.reshape(4, 4, 8, 128) * scale).reshape(4, 2, 16, 128).astype(BF16)


def side_by_side(x, y, mixed):
    low = lanes((8, 128)) < 64

    def half_turn(v):
        return pltpu.roll(v.reshape(512, 128), 64, axis=1).reshape(v.shape)

    first = jnp.where(low, x, half_turn(y))
    second = jnp.where(low, half_turn(x), y)
    both = jnp.stack([first, second], axis=3)
    both = both.transpose(0, 2, 1, 3, 4, 5, 6)
    mixed[...] = both.reshape(1024, 128)


def blocks_of(x):
    return x.astype(F32).reshape(2, 4, 2, 4, 8, 128)


def pairs_kernel(
    area, scene, recv, turned,
    lines, wide, staged, mate, table, src, z0, z1, z2, z3, lhs, own_power, res, landed, mixed, built,
    turn_sem, local_sem, read_sem, a_send, a_recv, b_send, b_recv, c_send, c_recv,
):
    zs = (z0, z1, z2, z3)
    lands = (recv.at[0], landed.at[0], landed.at[1], recv.at[1])
    k = lax.axis_index("region")
    acq = lax.axis_index("acq")
    z = acq // 4
    q = acq % 4
    xl, core = q // 2, q % 2
    right = (k, ((z + 1) % 4) * 4 + q)
    left = (k, ((z + 3) % 4) * 4 + q)

    def tile(j):
        return ((xl + j // 2) % 2) * 2 + (core + j % 2) % 2

    def rows16(start):
        return pl.ds(pl.multiple_of(start, 16), 16)

    barrier = pltpu.get_barrier_semaphore()
    for peer in (left, right):
        pl.semaphore_signal(barrier, inc=1, device_id=peer, device_id_type=MESH)

    for n in range(1, 32):
        o = ((k // 4 + n // 16) % 2) * 4 + (k + n // 4) % 4
        peer = (o, z * 4 + tile(n % 4))
        pl.semaphore_signal(barrier, inc=1, device_id=peer, device_id_type=MESH)

    reads = {}
    for j in (2, 3, 0, 1):
        columns = pl.ds(pl.multiple_of(tile(j) * 128, 128), 128)
        reads[j] = pltpu.make_async_copy(scene.at[:, :, :, columns], lines.at[j], read_sem.at[j])
        reads[j].start()
    for j in (2, 3):
        reads[j].wait()
        stage_columns(lines.at[j], wide.at[j], staged.at[j])
    pl.semaphore_wait(barrier, 33)

    def remote(from_ref, to_ref, send, recv, peer):
        return pltpu.make_async_remote_copy(
            src_ref=from_ref, dst_ref=to_ref, send_sem=send, recv_sem=recv,
            device_id=peer, device_id_type=MESH,
        )

    a_copies = {}

    def exchange(n, j, land):
        peer = (k, z * 4 + tile(j))
        a_copies[n] = remote(staged.at[j], land, a_send.at[n], a_recv.at[n], peer)
        a_copies[n].start()

    here16 = z0.at[:, rows16(q * 16), :]
    exchange(2, 2, here16)
    exchange(3, 3, here16)
    for j in (0, 1):
        reads[j].wait()
        stage_columns(lines.at[j], wide.at[j], staged.at[j])

    def near(j, side):
        return zs[1 + j // 2].at[:, rows16(side * 32 + ((core + j) % 2) * 16), :]

    b_copies = {}

    def send_along(j):
        data = staged.at[0] if j == 0 else zs[0].at[:, rows16(tile(j) * 16), :]
        for side, peer in ((0, right), (1, left)):
            n = side * 4 + j
            b_copies[j, side] = remote(data, near(j, side), b_send.at[n], b_recv.at[n], peer)
            b_copies[j, side].start()

    send_along(0)
    exchange(1, 1, here16)
    exchange(0, 1, mate)
    own = pltpu.make_async_copy(staged.at[0], here16, local_sem.at[1])
    own.start()
    sort_rows(area, table)
    sorted_rows = pltpu.make_async_copy(table, src, local_sem.at[0])
    sorted_rows.start()
    a_copies[1].wait_recv()
    send_along(1)
    a_copies[0].wait_recv()
    sorted_rows.wait()

    weights = column_weights()
    q64 = [pl.multiple_of(tile(j) * 64, 64) for j in range(4)]

    def build_near(w, _):
        build_own(w, src, weights, staged.at[0], q64[0], lhs)
        build_own(w, src, weights, mate, q64[1], lhs)
        return 0

    lax.fori_loop(0, 16, build_near, 0, unroll=2)
    relays = []

    def relay(j):
        side, peer = ((0, right), (1, left), (0, right), (1, left))[j]
        n = 8 + j
        relays.append(remote(
            near(j, side), zs[3].at[:, rows16(tile(j) * 16), :], b_send.at[n], b_recv.at[n], peer
        ))
        relays[-1].start()

    for j in (2, 3):
        a_copies[j].wait_recv()
        send_along(j)
    own.wait()

    def send_results(o, g):
        for j in (2, 3, 1, 0):
            p = tile(j)
            block, land = res.at[g, o * 4 + p], lands[g].at[k * 4 + q]
            away = remote(block, land, c_send.at[g], c_recv.at[g], (o, z * 4 + p))
            if j:
                away.start()
                continue

            @pl.when(o == k)
            def _():
                pltpu.make_async_copy(block, land, c_recv.at[g]).start()

            @pl.when(o != k)
            def _():
                away.start()

    def z0_tile(j):
        return z0.at[:, rows16(tile(j) * 16), :]

    def distant(n, u):
        x = (1 - (n // 2) * (1 - n // 3)) if u == 0 else (n % 2) * (1 - n // 3)
        y = 2 - (n + 1) // 2 if u == 0 else 2 + (n + 1) // 2
        return ((k // 4 + x) % 2) * 4 + (k + y) % 4

    def group(g):
        def windows(regions):
            pairs = [(o, o * 2 + h) for o in regions for h in range(2)]
            if g == 0:
                for _, w in pairs:
                    for j in (2, 3):
                        build_own(w, src, weights, z0_tile(j), q64[j], lhs)
            sums = [window_sums(w, src, weights, zs[g], lhs) for _, w in pairs]
            if g == 0:
                for (_, w), (_, intensity) in zip(pairs, sums):
                    own_intensities(w, intensity, own_power)
            for n, ((o, w), (full, intensity)) in enumerate(zip(pairs, sums)):
                h = n % 2
                block = coherence(full, intensity, own_power[w])
                res[g, pl.ds(o * 4, 4), h * 2 : h * 2 + 2] = block
                if h:
                    send_results(o, g)

        def step(n, _):
            windows([distant(n, 0), distant(n, 1)])
            return 0

        lax.fori_loop(0, 4, step, 0)

    group(0)
    for j in (0, 1):
        for side in range(2):
            b_copies[j, side].wait_recv()
    relay(0)
    relay(1)
    group(1)

    for j in (2, 3):
        b_copies[j, j - 2].wait_recv()
        relay(j)
    for j in (2, 3):
        b_copies[j, 3 - j].wait_recv()
    group(2)
    for copy in relays:
        copy.wait_recv()
    group(3)

    for g in (1, 2):
        pltpu.make_async_copy(res.at[g], lands[g], c_recv.at[g]).wait()

    def turn(n, _):
        same = blocks_of(landed[0, pl.ds(n * 8, 8)])
        cross = blocks_of(landed[1, pl.ds(n * 8, 8)])
        near = jnp.concatenate([same[:, 0:2], cross[:, 2:4]], axis=1)
        far = jnp.concatenate([cross[:, 0:2], same[:, 2:4]], axis=1)
        side_by_side(near, far, mixed)
        for i in range(8):
            y = mixed[pl.ds(i, 128, stride=8), :].T
            for x in range(2):
                for side in range(2):
                    for part in range(2):
                        lane = x * 64 + side * 32 + part * 8
                        pair = jnp.concatenate([y[lane : lane + 8], y[lane + 16 : lane + 24]], axis=0)
                        built[n, part, i, side, x * 16 : x * 16 + 16, :] = pair
        columns = pl.ds(pl.multiple_of(n * 128, 128), 128)
        pltpu.make_async_copy(
            built.at[n], turned.at[:, :, :, :, columns], turn_sem.at[n]
        ).start()
        return 0

    lax.fori_loop(0, 4, turn, 0)

    for copy in list(a_copies.values()) + list(b_copies.values()) + relays:
        copy.wait_send()
    for n in range(4):
        columns = pl.ds(n * 128, 128)
        pltpu.make_async_copy(
            built.at[n], turned.at[:, :, :, :, columns], turn_sem.at[n]
        ).wait()
    for g in range(4):
        some = pl.ds(0, 31)
        pltpu.make_async_copy(res.at[g, some], lands[g].at[some], c_send.at[g]).wait()
    for g in (0, 3):
        pltpu.make_async_copy(res.at[g], lands[g], c_recv.at[g]).wait()


def finish_kernel(recv, turned, out, built, mixed, write_sem, wide_sem):
    z = lax.axis_index("acq") // 4

    def rows_of(offset):
        return pl.ds(pl.multiple_of(((z + offset) % 4) * 32, 32), 32)

    copies = []

    def write(from_ref, to_ref, sem):
        copies.append(pltpu.make_async_copy(from_ref, to_ref, sem))
        copies[-1].start()

    for part in range(2):
        for d in range(2):
            land = out.at[part, :, rows_of(3 + 2 * d)]
            write(turned.at[part, :, d], land, wide_sem.at[part, d])
    for n in range(4):
        some = slice(n * 8, n * 8 + 8)
        side_by_side(blocks_of(recv[0, some]), blocks_of(recv[1, some]), mixed)
        for i in range(8):
            y = mixed[pl.ds(i, 128, stride=8), :].T
            for t in range(8):
                for part in range(2):
                    lane, at = t * 16 + part * 8, (t % 4) * 8
                    built[n, t // 4, part, i, at : at + 8, :] = y[lane : lane + 8]
        columns = pl.ds(n * 128, 128)
        for d in range(2):
            write(built.at[n, d], out.at[:, :, rows_of(2 * d), columns], write_sem.at[n, d])
    for copy in copies:
        copy.wait()


def local(scene_lines, assigned_area):
    smem = pl.BlockSpec(memory_space=pltpu.SMEM)
    vmem = pl.BlockSpec(memory_space=pltpu.VMEM)
    hbm = pl.BlockSpec(memory_space=pltpu.HBM)
    blocks = (4, 32, 4, 16, 128)
    got = pl.pallas_call(
        pairs_kernel,
        out_shape=[
            jax.ShapeDtypeStruct((2, 32, 4, 16, 128), BF16),
            jax.ShapeDtypeStruct((2, 8, 2, 32, 512), F32),
        ],
        in_specs=[smem, hbm],
        out_specs=[hbm, hbm],
        scratch_shapes=[
            pltpu.VMEM((4, 2, 8, 48, 128), BF16),
            pltpu.VMEM((4, 768, 128), F32),
            pltpu.VMEM((4, 48, 16, 128), BF16),
            pltpu.VMEM((48, 16, 128), BF16),
            pltpu.VMEM((2, 8, 128), jnp.int32),
            pltpu.SMEM((2, 8, 128), jnp.int32),
            pltpu.VMEM((48, 64, 128), BF16),
            pltpu.VMEM((48, 64, 128), BF16),
            pltpu.VMEM((48, 64, 128), BF16),
            pltpu.VMEM((48, 64, 128), BF16),
            pltpu.VMEM((16, 256, 512), BF16),
            pltpu.VMEM((16, 16, 8, 128), F32),
            pltpu.VMEM(blocks, BF16),
            pltpu.VMEM((2, 32, 4, 16, 128), BF16),
            pltpu.VMEM((1024, 128), F32),
            pltpu.VMEM((4, 2, 8, 2, 32, 128), F32),
            pltpu.SemaphoreType.DMA((4,)),
            pltpu.SemaphoreType.DMA((2,)),
            pltpu.SemaphoreType.DMA((4,)),
            pltpu.SemaphoreType.DMA((4,)),
            pltpu.SemaphoreType.DMA((4,)),
            pltpu.SemaphoreType.DMA((12,)),
            pltpu.SemaphoreType.DMA((12,)),
            pltpu.SemaphoreType.DMA((4,)),
            pltpu.SemaphoreType.DMA((4,)),
        ],
        compiler_params=pltpu.CompilerParams(
            vmem_limit_bytes=40 << 20, collective_id=0, has_side_effects=True
        ),
    )(
        pltpu.with_memory_space_constraint(assigned_area.reshape(1, 48), pltpu.HBM),
        pltpu.with_memory_space_constraint(scene_lines, pltpu.HBM),
    )
    return pl.pallas_call(
        finish_kernel,
        out_shape=jax.ShapeDtypeStruct((2, 8, 128, 512), F32),
        in_specs=[vmem, vmem],
        out_specs=hbm,
        scratch_shapes=[
            pltpu.VMEM((4, 2, 2, 8, 32, 128), F32),
            pltpu.VMEM((1024, 128), F32),
            pltpu.SemaphoreType.DMA((4, 2)),
            pltpu.SemaphoreType.DMA((2, 2)),
        ],
        compiler_params=pltpu.CompilerParams(vmem_limit_bytes=32 << 20),
    )(*got)


def solution(mesh):
    placed = (P(None, "acq", "region", None), P("region", None))
    return jax.shard_map(
        local, mesh=mesh, in_specs=placed, out_specs=P(None, "acq", None, "region"), check_vma=False
    )
```
